256 devices in a mesh: ctx: 32 (over z, x), head: 8 (over y, core).
Axes of the slice: x: 4, y: 4, z: 8, core: 2. Of those that a mesh axis runs over, the one named last changes fastest.
Arguments:
- queries: bfloat16 [16384, 8192], P('ctx', 'head'), may hold values from -6 to 6
- keys: bfloat16 [16384, 8192], P('ctx', 'head'), may hold values from -6 to 6
- values: bfloat16 [16384, 8192], P('ctx', 'head'), may hold values from -32 to 32, as said below
- gain: bfloat16 [8192], P('head'), may hold values from 0.25 to 1.75
- cotangent: bfloat16 [16384, 8192], P('ctx', 'head'), may hold values from -6 to 6
Outputs:
- normed: bfloat16 [16384, 8192], P('ctx', 'head')
- grad_queries: bfloat16 [16384, 8192], P('ctx', 'head')
- grad_keys: bfloat16 [16384, 8192], P('ctx', 'head')
- grad_values: bfloat16 [16384, 8192], P('ctx', 'head')
The draws below stay inside these ranges and needn't reach their ends.
Inputs may be any that keep to these rules, and one draw needn't show every extreme that they name: `values`: entries of a symmetric law, times a factor per column and a positive factor per token.
All inputs are finite; a program needn't handle non-finite values.
Results may differ from the reference program's by a relative error of at most 0.014.
Values may be sent and summed in bfloat16 or wider, within the bound.
No kernel may reach another device: no remote copies, remote signals or barrier semaphores. Data moves between devices by JAX's collectives and lax.ppermute only.
A program may use at most 128 MiB of HBM per device.

```python
import jax
import jax.numpy as jnp
from jax import lax

HEADS = 64
DH = 128
TOK_DEV = 512
TOKENS = 16384


def draw_values(key, part):
    key = jax.random.fold_in(key, 11)
    key_base, key_cols, key_rows = jax.random.split(key, 3)
    width = HEADS * DH
    columns = jnp.arange(width) // DH
    head_scale = 3.0 ** (columns.astype(jnp.float32) / (HEADS - 1))
    column_factor = jax.random.uniform(key_cols, (width,), jnp.float32, 0.7, 1.4)
    base = jnp.clip(jax.random.normal(key_base, (TOKENS, width), jnp.float32), -3.5, 3.5)
    row_scale = jax.random.uniform(key_rows, (TOKENS, 1), jnp.float32, 0.8, 1.25)
    base = base * row_scale
    return jnp.clip(base * head_scale * column_factor, -32.0, 32.0).astype(jnp.bfloat16)


def levels(stream_key, dims, shards, least, high):
    def one(dim, shards_of):
        draws = jax.random.uniform(jax.random.fold_in(jax.random.fold_in(stream_key, 6), dim), (shards_of,), jnp.float32, least / len(shards), high / len(shards))
        return jnp.repeat(jnp.exp(draws), dims[dim] // shards_of).reshape((-1,) + (1,) * (len(dims) - dim - 1))

    factor_of = one(*shards[0])
    for cut in shards[1:]:
        factor_of = factor_of * one(*cut)
    return factor_of


def noise(own_key, extent, scale, bound, pieces=(), held_as=jnp.bfloat16):
    factor_of = levels(own_key, extent, pieces, -0.22, 0.18) if pieces else 1.0
    values = jax.random.normal(own_key, extent, jnp.float32) * scale * factor_of
    return jnp.minimum(jnp.maximum(values, -bound), bound).astype(held_as)


def setup_inputs(seed: int = 0) -> dict:
    splits = jax.random.split(jax.random.key(seed), 6)
    return {
        "queries": noise(splits[0], (TOKENS, HEADS * DH), 1.0, 6.0, ((0, 32), (1, 8))),
        "keys": noise(splits[1], (TOKENS, HEADS * DH), 1.0, 6.0, ((0, 32), (1, 8))),
        "values": draw_values(jax.random.fold_in(splits[5], 71), 0),
        "gain": jnp.clip(1.0 + 0.15 * jax.random.normal(splits[3], (HEADS * DH,), jnp.float32), 0.25, 1.75).astype(jnp.bfloat16),
        "cotangent": noise(splits[4], (TOKENS, HEADS * DH), 1.0, 6.0, ((0, 32), (1, 8))),
    }


def round_keep(array):
    return lax.optimization_barrier(array.astype(jnp.bfloat16)).astype(jnp.float32)

def reference(queries, keys, values, gain, cotangent):
    count = TOKENS // TOK_DEV
    width = HEADS * DH
    block_shape = (count, TOK_DEV, HEADS, DH)
    q_blocks = queries.reshape(block_shape)
    k_blocks = keys.reshape(block_shape)
    v_blocks = values.reshape(block_shape)
    positions = jnp.arange(TOK_DEV)
    causal = positions[:, None] >= positions[None, :]

    def forward_step(running, blocks):
        q_part, k_part, v_part = [x.astype(jnp.float32) for x in blocks]
        scores = jnp.einsum('thd,shd->hts', q_part, k_part)
        attn = round_keep(jnp.where(causal[None], scores, 0.0))
        state_bf = round_keep(running)
        attended = jnp.einsum('hts,shd->thd', attn, v_part) + jnp.einsum('thd,hde->the', q_part, state_bf)
        updated = running + jnp.einsum('thd,the->hde', k_part, v_part)
        return (updated, (attended, running))
    start_state = jnp.zeros((HEADS, DH, DH), jnp.float32)
    final_state, (attended, prefixes) = lax.scan(forward_step, start_state, (q_blocks, k_blocks, v_blocks))
    attended = attended.reshape(TOKENS, width)
    gain_f = gain.astype(jnp.float32)
    inv_rms = lax.rsqrt(lax.optimization_barrier(jnp.sum(attended * attended, axis=1)) / width + 1e-06)
    normed = (attended * inv_rms[:, None] * gain_f).astype(jnp.bfloat16)
    scaled = cotangent.astype(jnp.float32) * gain_f
    cross = lax.optimization_barrier(jnp.sum(scaled * attended, axis=1)) / width
    grad_att = (inv_rms[:, None] * scaled - attended * (inv_rms ** 3 * cross)[:, None]).astype(jnp.bfloat16)
    g_blocks = grad_att.reshape(block_shape)

    def backward_step(running, blocks):
        q_part, k_part, v_part, g_part, prefix = blocks
        q_part, k_part, v_part, g_part = [x.astype(jnp.float32) for x in (q_part, k_part, v_part, g_part)]
        scores = jnp.einsum('thd,shd->hts', q_part, k_part)
        attn = round_keep(jnp.where(causal[None], scores, 0.0))
        state_bf = round_keep(prefix)
        later_bf = round_keep(running)
        grad_scores = jnp.einsum('thd,shd->hts', g_part, v_part)
        grad_attn = round_keep(jnp.where(causal[None], grad_scores, 0.0))
        grad_q = jnp.einsum('hts,shd->thd', grad_attn, k_part) + jnp.einsum('the,hde->thd', g_part, state_bf)
        grad_k = jnp.einsum('hts,thd->shd', grad_attn, q_part) + jnp.einsum('the,hde->thd', v_part, later_bf)
        grad_v = jnp.einsum('hts,thd->shd', attn, g_part) + jnp.einsum('thd,hde->the', k_part, later_bf)
        updated = running + jnp.einsum('thd,the->hde', q_part, g_part)
        return (updated, (grad_q.astype(jnp.bfloat16), grad_k.astype(jnp.bfloat16), grad_v.astype(jnp.bfloat16)))
    last_state, (grad_q, grad_k, grad_v) = lax.scan(backward_step, start_state, (q_blocks, k_blocks, v_blocks, g_blocks, prefixes), reverse=True)
    return (normed, grad_q.reshape(TOKENS, width), grad_k.reshape(TOKENS, width), grad_v.reshape(TOKENS, width))
```

```python
import functools

import jax
import jax.numpy as jnp
from jax import lax
from jax.experimental import pallas as pl
from jax.experimental.pallas import tpu as pltpu
from jax.sharding import PartitionSpec as P

DH = 128
F32 = jnp.float32
BF16 = jnp.bfloat16
VMEM_LIMIT = 48 * 1024 * 1024

NT = (((1,), (1,)), ((), ()))
NN = (((1,), (0,)), ((), ()))
TN = (((0,), (0,)), ((), ()))


def dot(a, b, dims):
    return lax.dot_general(a, b, dims, preferred_element_type=F32)


def params(*axes):
    return pltpu.CompilerParams(dimension_semantics=axes, vmem_limit_bytes=VMEM_LIMIT)


def outer_kernel(a_ref, b_ref, out_ref):
    for h in range(a_ref.shape[1] // DH):
        cols = slice(h * DH, (h + 1) * DH)
        out_ref[cols, :] = dot(a_ref[:, cols], b_ref[:, cols], TN).astype(BF16)


def outer(a, b, step):
    rows, width = a.shape
    spec = pl.BlockSpec((rows, step), lambda i: (0, i))
    return pl.pallas_call(
        outer_kernel,
        grid=(width // step,),
        in_specs=[spec, spec],
        out_specs=pl.BlockSpec((step, DH), lambda i: (i, 0)),
        out_shape=jax.ShapeDtypeStruct((width, DH), BF16),
        compiler_params=params("arbitrary"),
        name="outer",
    )(a, b)


def scan_kernel(x_ref, out_ref, *, backward):
    count = x_ref.shape[0]
    total = jnp.zeros(x_ref.shape[1:], F32)
    for lap in range(count):
        i = count - 1 - lap if backward else lap
        out_ref[i] = total.astype(BF16)
        total = total + x_ref[i].astype(F32)


def scan(x, backward):
    return pl.pallas_call(
        functools.partial(scan_kernel, backward=backward),
        out_shape=jax.ShapeDtypeStruct(x.shape, BF16),
        compiler_params=params(),
        name="suffix" if backward else "prefix",
    )(x)


def exchange(x, axis):
    return lax.all_to_all(x, axis, 0, 0)


def running(local, backward):
    count = lax.axis_size("ctx")
    parts = local.reshape(count, local.shape[0] // count, DH)
    mine = scan(exchange(parts, "ctx"), backward)
    return exchange(mine, "ctx").reshape(local.shape)


def keep_lower(x):
    row = lax.broadcasted_iota(jnp.int32, x.shape, 0)
    col = lax.broadcasted_iota(jnp.int32, x.shape, 1)
    return jnp.where(row >= col, x, 0.0)


def keep_upper(x):
    row = lax.broadcasted_iota(jnp.int32, x.shape, 0)
    col = lax.broadcasted_iota(jnp.int32, x.shape, 1)
    return jnp.where(row <= col, x, 0.0)


def lower_product(a, b, c):
    half = a.shape[0] // 2
    top = keep_lower(dot(a[:half], b[:half], NT)).astype(BF16)
    low = dot(a[half:], b[:half], NT).astype(BF16)
    last = keep_lower(dot(a[half:], b[half:], NT)).astype(BF16)
    return dot(top, c[:half], NN), dot(low, c[:half], NN) + dot(last, c[half:], NN)


def upper_product(a, b, c):
    half = a.shape[0] // 2
    top = keep_upper(dot(a[:half], b[:half], NT)).astype(BF16)
    high = dot(a[:half], b[half:], NT).astype(BF16)
    last = keep_upper(dot(a[half:], b[half:], NT)).astype(BF16)
    return dot(top, c[:half], NN) + dot(high, c[half:], NN), dot(last, c[half:], NN)


def within_kernel(q_ref, k_ref, v_ref, out_ref):
    half = q_ref.shape[0] // 2
    one, two = lower_product(q_ref[...], k_ref[...], v_ref[...])
    out_ref[:half] = one
    out_ref[half:] = two


def within(q, k, v):
    rows, width = q.shape
    spec = pl.BlockSpec((rows, DH), lambda i: (0, i))
    return pl.pallas_call(
        within_kernel,
        grid=(width // DH,),
        in_specs=[spec] * 3,
        out_specs=spec,
        out_shape=jax.ShapeDtypeStruct((rows, width), F32),
        compiler_params=params("arbitrary"),
        name="within",
    )(q, k, v)


def attend_kernel(a_ref, q_ref, s_ref, cot_ref, gain_ref, att_ref, stat_ref, sq_ref, cr_ref):
    step = pl.program_id(0)

    @pl.when(step == 0)
    def _():
        sq_ref[...] = jnp.zeros_like(sq_ref)
        cr_ref[...] = jnp.zeros_like(cr_ref)

    for h in range(q_ref.shape[1] // DH):
        cols = slice(h * DH, (h + 1) * DH)
        att = a_ref[:, cols] + dot(q_ref[:, cols], s_ref[cols, :], NN)
        att_ref[:, cols] = att
        scaled = cot_ref[:, cols].astype(F32) * gain_ref[:, cols].astype(F32)
        sq_ref[...] += att * att
        cr_ref[...] += scaled * att

    @pl.when(step == pl.num_programs(0) - 1)
    def _():
        blocks = sq_ref.shape[0] // DH
        for i in range(blocks):
            rows = slice(i * DH, (i + 1) * DH)
            for j, ref in enumerate((sq_ref, cr_ref)):
                line = jnp.sum(ref[rows, :].T, axis=0, keepdims=True)
                for copy in range(stat_ref.shape[0]):
                    stat_ref[copy, j * blocks + i : j * blocks + i + 1, :] = line


def attend(a, q, s, cot, gain, copies, step):
    rows, width = q.shape
    lines = 2 * rows // DH
    spec = pl.BlockSpec((rows, step), lambda i: (0, i))
    return pl.pallas_call(
        attend_kernel,
        grid=(width // step,),
        in_specs=[
            spec,
            spec,
            pl.BlockSpec((step, DH), lambda i: (i, 0)),
            spec,
            pl.BlockSpec((1, step), lambda i: (0, i)),
        ],
        out_specs=[spec, pl.BlockSpec((copies, lines, DH), lambda i: (0, 0, 0))],
        out_shape=[
            jax.ShapeDtypeStruct((rows, width), F32),
            jax.ShapeDtypeStruct((copies, lines, DH), F32),
        ],
        scratch_shapes=[pltpu.VMEM((rows, DH), F32), pltpu.VMEM((rows, DH), F32)],
        compiler_params=params("arbitrary"),
        name="attend",
    )(a, q, s, cot, gain)


def grad_kernel(att_ref, cot_ref, gain_ref, stat_ref, q_ref, g_ref, lg_ref, rms_ref, r_ref, c_ref, *, total):
    rows = att_ref.shape[0]

    @pl.when(pl.program_id(0) == 0)
    def _():
        blocks = rows // DH
        stats = jnp.sum(stat_ref[...], axis=0) / total
        for i in range(blocks):
            span = slice(i * DH, (i + 1) * DH)
            inv = lax.rsqrt(stats[i : i + 1, :] + 1e-06)
            cross = stats[blocks + i : blocks + i + 1, :]
            inv_tile = jnp.broadcast_to(inv, (DH, DH)).T
            r_ref[span, :] = inv_tile
            rms_ref[span, :] = inv_tile
            c_ref[span, :] = jnp.broadcast_to(inv**3 * cross, (DH, DH)).T

    for h in range(q_ref.shape[1] // DH):
        cols = slice(h * DH, (h + 1) * DH)
        scaled = cot_ref[:, cols].astype(F32) * gain_ref[:, cols].astype(F32)
        g = (r_ref[...] * scaled - att_ref[:, cols] * c_ref[...]).astype(BF16)
        g_ref[:, cols] = g
        lg_ref[cols, :] = dot(q_ref[:, cols], g, TN).astype(BF16)


def grad(att, cot, gain, stats, q, total, step):
    rows, width = q.shape
    spec = pl.BlockSpec((rows, step), lambda i: (0, i))
    return pl.pallas_call(
        functools.partial(grad_kernel, total=total),
        grid=(width // step,),
        in_specs=[
            spec,
            spec,
            pl.BlockSpec((1, step), lambda i: (0, i)),
            pl.BlockSpec(stats.shape, lambda i: (0, 0, 0)),
            spec,
        ],
        out_specs=[spec, pl.BlockSpec((step, DH), lambda i: (i, 0)), pl.BlockSpec((rows, DH), lambda i: (0, 0))],
        out_shape=[
            jax.ShapeDtypeStruct((rows, width), BF16),
            jax.ShapeDtypeStruct((width, DH), BF16),
            jax.ShapeDtypeStruct((rows, DH), F32),
        ],
        scratch_shapes=[pltpu.VMEM((rows, DH), F32), pltpu.VMEM((rows, DH), F32)],
        compiler_params=params("arbitrary"),
        name="grad",
    )(att, cot, gain, stats, q)


def side_kernel(q_ref, k_ref, v_ref, g_ref, s_ref, att_ref, gain_ref, rms_ref, n_ref, gq_ref, gk_ref, gv_ref):
    half = q_ref.shape[0] // 2
    q, k, v, g = q_ref[...], k_ref[...], v_ref[...], g_ref[...]
    n_ref[...] = (att_ref[...] * rms_ref[...] * gain_ref[...].astype(F32)).astype(BF16)
    one, two = lower_product(g, v, k)
    far = dot(g, s_ref[...], NT)
    gq_ref[:half] = (one + far[:half]).astype(BF16)
    gq_ref[half:] = (two + far[half:]).astype(BF16)
    one, two = upper_product(v, g, q)
    gk_ref[:half] = one
    gk_ref[half:] = two
    one, two = upper_product(k, q, g)
    gv_ref[:half] = one
    gv_ref[half:] = two


def side(q, k, v, g, s, att, gain, rms):
    rows, width = q.shape
    spec = pl.BlockSpec((rows, DH), lambda i: (0, i))
    return pl.pallas_call(
        side_kernel,
        grid=(width // DH,),
        in_specs=[
            spec,
            spec,
            spec,
            spec,
            pl.BlockSpec((DH, DH), lambda i: (i, 0)),
            spec,
            pl.BlockSpec((1, DH), lambda i: (0, i)),
            pl.BlockSpec((rows, DH), lambda i: (0, 0)),
        ],
        out_specs=[spec] * 4,
        out_shape=[
            jax.ShapeDtypeStruct((rows, width), BF16),
            jax.ShapeDtypeStruct((rows, width), BF16),
            jax.ShapeDtypeStruct((rows, width), F32),
            jax.ShapeDtypeStruct((rows, width), F32),
        ],
        compiler_params=params("arbitrary"),
        name="side",
    )(q, k, v, g, s, att, gain, rms)


def last_kernel(gk_ref, gv_ref, k_ref, v_ref, s_ref, outk_ref, outv_ref):
    for h in range(k_ref.shape[1] // DH):
        cols = slice(h * DH, (h + 1) * DH)
        s = s_ref[cols, :]
        outk_ref[:, cols] = (gk_ref[:, cols] + dot(v_ref[:, cols], s, NT)).astype(BF16)
        outv_ref[:, cols] = (gv_ref[:, cols] + dot(k_ref[:, cols], s, NN)).astype(BF16)


def last(gk, gv, k, v, s, step):
    rows, width = k.shape
    spec = pl.BlockSpec((rows, step), lambda i: (0, i))
    return pl.pallas_call(
        last_kernel,
        grid=(width // step,),
        in_specs=[spec] * 4 + [pl.BlockSpec((step, DH), lambda i: (i, 0))],
        out_specs=[spec] * 2,
        out_shape=[jax.ShapeDtypeStruct((rows, width), BF16)] * 2,
        compiler_params=params("arbitrary"),
        name="last",
    )(gk, gv, k, v, s)


def body(queries, keys, values, gain, cotangent):
    rows, width = queries.shape
    heads = lax.axis_size("head")
    gain = gain.reshape(1, width)
    state = running(outer(keys, values, 256), False)
    a = within(queries, keys, values)
    att, stats = attend(a, queries, state, cotangent, gain, heads, 256)
    stats = exchange(stats, "head")
    g, local_grad, rms = grad(att, cotangent, gain, stats, queries, width * heads, 256)
    later = running(local_grad, True)
    normed, grad_q, gk, gv = side(queries, keys, values, g, state, att, gain, rms)
    grad_k, grad_v = last(gk, gv, keys, values, later, 256)
    return normed, grad_q, grad_k, grad_v


def solution(mesh):
    return jax.shard_map(
        body,
        mesh=mesh,
        in_specs=(
            P("ctx", "head"),
            P("ctx", "head"),
            P("ctx", "head"),
            P("head"),
            P("ctx", "head"),
        ),
        out_specs=(P("ctx", "head"), P("ctx", "head"), P("ctx", "head"), P("ctx", "head")),
        check_vma=False,
    )
```

```python
import functools

import jax
import jax.numpy as jnp
from jax import lax
from jax.experimental import pallas as pl
from jax.experimental.pallas import tpu as pltpu
from jax.sharding import PartitionSpec as P

DH = 128
F32 = jnp.float32
BF16 = jnp.bfloat16
VMEM_LIMIT = 16 * 1024 * 1024
VMEM_MOST = 60 * 1024 * 1024
VMEM = pl.BlockSpec(memory_space=pltpu.VMEM)


def far(x):
    return pltpu.with_memory_space_constraint(x, pltpu.HBM)


NT = (((1,), (1,)), ((), ()))
NN = (((1,), (0,)), ((), ()))
TN = (((0,), (0,)), ((), ()))


def dot(a, b, dims):
    return lax.dot_general(a, b, dims, preferred_element_type=F32)


def params(limit=VMEM_LIMIT):
    return pltpu.CompilerParams(vmem_limit_bytes=limit)


def heads_of(ref):
    return [slice(c, c + DH) for c in range(0, ref.shape[1], DH)]


HBM = pl.BlockSpec(memory_space=pltpu.HBM)


class Mover:
    def __init__(self, sems):
        self.sems = sems
        self.used = 0

    def start(self, src, dst):
        copy = pltpu.make_async_copy(src, dst, self.sems.at[self.used])
        self.used += 1
        copy.start()
        return copy


def chunks_of(ref, step):
    return [slice(r, r + step) for r in range(0, ref.shape[0], step)]


def groups_of(ref, step):
    return [slice(c, c + step) for c in range(0, ref.shape[1], step)]


def outer_kernel(a_hbm, b_hbm, out_hbm, a_ref, b_ref, acc_ref, out_ref, sems, *, step):
    mover = Mover(sems)
    chunks = chunks_of(a_ref, step)
    loads = [
        (mover.start(a_hbm.at[rows], a_ref.at[rows]), mover.start(b_hbm.at[rows], b_ref.at[rows])) for rows in chunks
    ]
    for i, rows in enumerate(chunks):
        for copy in loads[i]:
            copy.wait()
        for cols in heads_of(a_ref):
            term = dot(a_ref[rows, cols], b_ref[rows, cols], TN)
            if i > 0:
                term = acc_ref[cols, :] + term
            if i < len(chunks) - 1:
                acc_ref[cols, :] = term
            else:
                out_ref[cols, :] = term.astype(BF16)
    mover.start(out_ref, out_hbm).wait()


def outer(a, b, step):
    rows, width = a.shape
    return pl.pallas_call(
        functools.partial(outer_kernel, step=step),
        in_specs=[HBM] * 2,
        out_specs=HBM,
        out_shape=pltpu.HBM((width, DH), BF16),
        scratch_shapes=[
            pltpu.VMEM((rows, width), BF16),
            pltpu.VMEM((rows, width), BF16),
            pltpu.VMEM((width, DH), F32),
            pltpu.VMEM((width, DH), BF16),
            pltpu.SemaphoreType.DMA((2 * rows // step + 1,)),
        ],
        compiler_params=params(VMEM_MOST),
        name="outer",
    )(far(a), far(b))


def scan_kernel(x_ref, out_ref, *, backward):
    count = x_ref.shape[0]
    total = jnp.zeros(x_ref.shape[1:], F32)
    for lap in range(count):
        i = count - 1 - lap if backward else lap
        out_ref[i] = total.astype(BF16)
        total = total + x_ref[i].astype(F32)


def scan(x, backward):
    return pl.pallas_call(
        functools.partial(scan_kernel, backward=backward),
        out_shape=jax.ShapeDtypeStruct(x.shape, BF16),
        compiler_params=params(),
        name="suffix" if backward else "prefix",
    )(x)


def exchange(x, axis):
    return lax.all_to_all(x, axis, 0, 0)


def keep_lower(x):
    row = lax.broadcasted_iota(jnp.int32, x.shape, 0)
    col = lax.broadcasted_iota(jnp.int32, x.shape, 1)
    return jnp.where(row >= col, x, 0.0)


def keep_upper(x):
    row = lax.broadcasted_iota(jnp.int32, x.shape, 0)
    col = lax.broadcasted_iota(jnp.int32, x.shape, 1)
    return jnp.where(row <= col, x, 0.0)


def lower_product(a, b, c):
    half = a.shape[0] // 2
    top = keep_lower(dot(a[:half], b[:half], NT)).astype(BF16)
    low = dot(a[half:], b[:half], NT).astype(BF16)
    last = keep_lower(dot(a[half:], b[half:], NT)).astype(BF16)
    return dot(top, c[:half], NN), dot(low, c[:half], NN) + dot(last, c[half:], NN)


def upper_product(a, b, c):
    half = a.shape[0] // 2
    top = keep_upper(dot(a[:half], b[:half], NT)).astype(BF16)
    high = dot(a[:half], b[half:], NT).astype(BF16)
    last = keep_upper(dot(a[half:], b[half:], NT)).astype(BF16)
    return dot(top, c[:half], NN) + dot(high, c[half:], NN), dot(last, c[half:], NN)


def within_kernel(q_hbm, k_hbm, v_hbm, out_hbm, q_ref, k_ref, v_ref, out_ref, sems):
    mover = Mover(sems)
    half = q_ref.shape[0] // 2
    loads = [mover.start(src, dst) for src, dst in ((q_hbm, q_ref), (k_hbm, k_ref), (v_hbm, v_ref))]
    for copy in loads:
        copy.wait()
    for cols in heads_of(q_ref):
        one, two = lower_product(q_ref[:, cols], k_ref[:, cols], v_ref[:, cols])
        out_ref[:half, cols] = one
        out_ref[half:, cols] = two
    mover.start(out_ref, out_hbm).wait()


def within(q, k, v):
    return pl.pallas_call(
        within_kernel,
        in_specs=[HBM] * 3,
        out_specs=HBM,
        out_shape=pltpu.HBM(q.shape, F32),
        scratch_shapes=[pltpu.VMEM(q.shape, BF16)] * 3 + [pltpu.VMEM(q.shape, F32), pltpu.SemaphoreType.DMA((4,))],
        compiler_params=params(VMEM_MOST),
        name="within",
    )(far(q), far(k), far(v))


def attend_kernel(a_hbm, q_ref, s_ref, cot_ref, gain_ref, att_ref, stat_ref, a_ref, sems):
    mover = Mover(sems)
    rows = q_ref.shape[0]
    chunks = chunks_of(q_ref, DH)
    loads = [mover.start(a_hbm.at[span], a_ref.at[span]) for span in chunks]
    for cols in heads_of(q_ref):
        att_ref[:, cols] = dot(q_ref[:, cols], s_ref[cols, :], NN)
    for i, span in enumerate(chunks):
        loads[i].wait()
        sq = jnp.zeros((DH, DH), F32)
        cr = jnp.zeros((DH, DH), F32)
        for cols in heads_of(q_ref):
            att = a_ref[span, cols] + att_ref[span, cols]
            att_ref[span, cols] = att
            scaled = cot_ref[span, cols].astype(F32) * gain_ref[:, cols].astype(F32)
            sq += att * att
            cr += scaled * att
        for j, part in enumerate((sq, cr)):
            line = jnp.sum(part.T, axis=0, keepdims=True)
            for copy in range(stat_ref.shape[0]):
                stat_ref[copy, j * len(chunks) + i : j * len(chunks) + i + 1, :] = line


def attend(a, q, s, cot, gain, copies):
    rows, width = q.shape
    vmem = pl.BlockSpec(memory_space=pltpu.VMEM)
    return pl.pallas_call(
        attend_kernel,
        in_specs=[HBM] + [vmem] * 4,
        out_shape=[
            jax.ShapeDtypeStruct((rows, width), F32),
            jax.ShapeDtypeStruct((copies, 2 * rows // DH, DH), F32),
        ],
        scratch_shapes=[pltpu.VMEM((rows, width), F32), pltpu.SemaphoreType.DMA((rows // DH,))],
        compiler_params=params(),
        name="attend",
    )(far(a), q, s, cot, gain)


def grad_kernel(
    att_ref, cot_ref, gain_ref, stat_ref, q_ref, g_hbm, lg_hbm, n_hbm, g_ref, lg_ref, n_ref, sems, *, total
):
    mover = Mover(sems)
    rows = att_ref.shape[0]
    blocks = rows // DH
    stats = jnp.sum(stat_ref[...], axis=0) / total
    inv = lax.rsqrt(stats[:blocks] + 1e-06)
    pull = inv**3 * stats[blocks:]
    stores = []
    for i, span in enumerate(chunks_of(att_ref, DH)):
        inv_tile = jnp.broadcast_to(inv[i : i + 1], (DH, DH)).T
        pull_tile = jnp.broadcast_to(pull[i : i + 1], (DH, DH)).T
        for cols in heads_of(q_ref):
            gain = gain_ref[:, cols].astype(F32)
            att = att_ref[span, cols]
            scaled = cot_ref[span, cols].astype(F32) * gain
            g_ref[span, cols] = (inv_tile * scaled - att * pull_tile).astype(BF16)
            n_ref[span, cols] = (att * inv_tile * gain).astype(BF16)
        stores.append(mover.start(g_ref.at[span], g_hbm.at[span]))
        stores.append(mover.start(n_ref.at[span], n_hbm.at[span]))
    for cols in heads_of(q_ref):
        lg_ref[cols, :] = dot(q_ref[:, cols], g_ref[:, cols], TN).astype(BF16)
    stores.append(mover.start(lg_ref, lg_hbm))
    for copy in stores:
        copy.wait()


def grad(att, cot, gain, stats, q, total):
    rows, width = q.shape
    shapes = [(rows, width), (width, DH), (rows, width)]
    return pl.pallas_call(
        functools.partial(grad_kernel, total=total),
        out_specs=[HBM] * 3,
        out_shape=[pltpu.HBM(shape, BF16) for shape in shapes],
        scratch_shapes=[pltpu.VMEM(shape, BF16) for shape in shapes]
        + [pltpu.SemaphoreType.DMA((2 * rows // DH + 1,))],
        compiler_params=params(),
        name="grad",
    )(att, cot, gain, stats, q)


def side_kernel(q_hbm, k_hbm, v_hbm, g_hbm, s_hbm, *refs, step):
    gq_hbm, gk_hbm, gv_hbm, q_ref, k_ref, v_ref, g_ref, s_ref, gq_ref, gk_ref, gv_ref, sems = refs
    mover = Mover(sems)
    half = q_ref.shape[0] // 2
    groups = groups_of(q_ref, step)
    here = step // DH
    s_in = mover.start(s_hbm, s_ref)
    pairs = ((g_hbm, g_ref), (v_hbm, v_ref), (k_hbm, k_ref), (q_hbm, q_ref))
    loads = [[mover.start(src.at[:, group], dst.at[:, group]) for src, dst in pairs] for group in groups]
    stores = []
    s_in.wait()
    for i, group in enumerate(groups):
        for copy in loads[i]:
            copy.wait()
        spans = heads_of(q_ref)[i * here : (i + 1) * here]
        for cols in spans:
            one, two = upper_product(v_ref[:, cols], g_ref[:, cols], q_ref[:, cols])
            gk_ref[:half, cols] = one
            gk_ref[half:, cols] = two
        stores.append(mover.start(gk_ref.at[:, group], gk_hbm.at[:, group]))
        for cols in spans:
            one, two = upper_product(k_ref[:, cols], q_ref[:, cols], g_ref[:, cols])
            gv_ref[:half, cols] = one
            gv_ref[half:, cols] = two
        stores.append(mover.start(gv_ref.at[:, group], gv_hbm.at[:, group]))
        for cols in spans:
            g = g_ref[:, cols]
            one, two = lower_product(g, v_ref[:, cols], k_ref[:, cols])
            rest = dot(g, s_ref[cols, :], NT)
            gq_ref[:half, cols] = (one + rest[:half]).astype(BF16)
            gq_ref[half:, cols] = (two + rest[half:]).astype(BF16)
        stores.append(mover.start(gq_ref.at[:, group], gq_hbm.at[:, group]))
    for copy in stores:
        copy.wait()


def side(q, k, v, g, s, step):
    outs = [pltpu.HBM(q.shape, kind) for kind in (BF16, F32, F32)]
    ins = (q, k, v, g, s)
    return pl.pallas_call(
        functools.partial(side_kernel, step=step),
        in_specs=[HBM] * len(ins),
        out_specs=[HBM] * len(outs),
        out_shape=outs,
        scratch_shapes=[pltpu.VMEM(x.shape, x.dtype) for x in (*ins, *outs)]
        + [pltpu.SemaphoreType.DMA((1 + 7 * q.shape[1] // step,))],
        compiler_params=params(VMEM_MOST),
        name="side",
    )(*[far(x) for x in ins])


def last_kernel(gk_hbm, gv_hbm, k_ref, v_ref, s_ref, outk_hbm, outv_hbm, gk_ref, gv_ref, outk_ref, outv_ref, sems, *, step):
    mover = Mover(sems)
    chunks = chunks_of(k_ref, step)
    loads = [
        (mover.start(gk_hbm.at[rows], gk_ref.at[rows]), mover.start(gv_hbm.at[rows], gv_ref.at[rows]))
        for rows in chunks
    ]
    stores = []
    for i, rows in enumerate(chunks):
        loads[i][0].wait()
        for cols in heads_of(k_ref):
            far = dot(v_ref[rows, cols], s_ref[cols, :], NT)
            outk_ref[rows, cols] = (gk_ref[rows, cols] + far).astype(BF16)
        stores.append(mover.start(outk_ref.at[rows], outk_hbm.at[rows]))
        loads[i][1].wait()
        for cols in heads_of(k_ref):
            far = dot(k_ref[rows, cols], s_ref[cols, :], NN)
            outv_ref[rows, cols] = (gv_ref[rows, cols] + far).astype(BF16)
        stores.append(mover.start(outv_ref.at[rows], outv_hbm.at[rows]))
    for copy in stores:
        copy.wait()


def last(gk, gv, k, v, s, step):
    rows, width = k.shape
    vmem = pl.BlockSpec(memory_space=pltpu.VMEM)
    return pl.pallas_call(
        functools.partial(last_kernel, step=step),
        in_specs=[HBM] * 2 + [vmem] * 3,
        out_specs=[HBM] * 2,
        out_shape=[jax.ShapeDtypeStruct((rows, width), BF16)] * 2,
        scratch_shapes=[pltpu.VMEM((rows, width), F32)] * 2
        + [pltpu.VMEM((rows, width), BF16)] * 2
        + [pltpu.SemaphoreType.DMA((4 * rows // step,))],
        compiler_params=params(),
        name="last",
    )(far(gk), far(gv), k, v, s)


def body(queries, keys, values, gain, cotangent):
    rows, width = queries.shape
    count, heads = lax.axis_size("ctx"), lax.axis_size("head")
    gain = gain.reshape(1, width)
    parts = (count, width // count, DH)

    local = exchange(outer(keys, values, 256).reshape(parts), "ctx")
    a = within(queries, keys, values)
    local, a, gain = lax.optimization_barrier((local, a, gain))
    state = exchange(scan(local, False), "ctx").reshape(width, DH)

    att, stats = attend(a, queries, state, cotangent, gain, heads)
    stats = exchange(stats, "head")
    g, local, normed = grad(att, cotangent, gain, stats, queries, width * heads)

    local = exchange(local.reshape(parts), "ctx")
    sides = side(queries, keys, values, g, state, 256)
    local, grad_q, gk, gv = lax.optimization_barrier((local, *sides))
    later = exchange(scan(local, True), "ctx").reshape(width, DH)
    grad_k, grad_v = last(gk, gv, keys, values, later, 256)
    return normed, grad_q, grad_k, grad_v


def solution(mesh):
    return jax.shard_map(
        body,
        mesh=mesh,
        in_specs=(
            P("ctx", "head"),
            P("ctx", "head"),
            P("ctx", "head"),
            P("head"),
            P("ctx", "head"),
        ),
        out_specs=(P("ctx", "head"), P("ctx", "head"), P("ctx", "head"), P("ctx", "head")),
        check_vma=False,
    )
```

```python
import functools

import jax
import jax.numpy as jnp
from jax import lax
from jax.experimental import pallas as pl
from jax.experimental.pallas import tpu as pltpu
from jax.sharding import PartitionSpec as P

DH = 128
F32 = jnp.float32
BF16 = jnp.bfloat16
PART = F32
SCAN_COST = 10_000_000_000
VMEM_LIMIT = 16 * 1024 * 1024
VMEM_MOST = 60 * 1024 * 1024
VMEM = pl.BlockSpec(memory_space=pltpu.VMEM)


def far(x):
    return pltpu.with_memory_space_constraint(x, pltpu.HBM)


NT = (((1,), (1,)), ((), ()))
NN = (((1,), (0,)), ((), ()))
TN = (((0,), (0,)), ((), ()))


def dot(a, b, dims):
    return lax.dot_general(a, b, dims, preferred_element_type=F32)


def params(limit=VMEM_LIMIT):
    return pltpu.CompilerParams(vmem_limit_bytes=limit)


def heads_of(ref):
    return [slice(c, c + DH) for c in range(0, ref.shape[1], DH)]


HBM = pl.BlockSpec(memory_space=pltpu.HBM)


class Mover:
    def __init__(self, sems):
        self.sems = sems
        self.used = 0

    def start(self, src, dst):
        copy = pltpu.make_async_copy(src, dst, self.sems.at[self.used])
        self.used += 1
        copy.start()
        return copy


def chunks_of(ref, step):
    return [slice(r, r + step) for r in range(0, ref.shape[0], step)]


def groups_of(ref, step):
    return [slice(c, c + step) for c in range(0, ref.shape[1], step)]


def outer_kernel(a_hbm, b_hbm, out_hbm, a_ref, b_ref, acc_ref, out_ref, sems, *, step):
    mover = Mover(sems)
    chunks = chunks_of(a_ref, step)
    loads = [
        (mover.start(a_hbm.at[rows], a_ref.at[rows]), mover.start(b_hbm.at[rows], b_ref.at[rows])) for rows in chunks
    ]
    for i, rows in enumerate(chunks):
        for copy in loads[i]:
            copy.wait()
        for cols in heads_of(a_ref):
            term = dot(a_ref[rows, cols], b_ref[rows, cols], TN)
            if i > 0:
                term = acc_ref[cols, :] + term
            if i < len(chunks) - 1:
                acc_ref[cols, :] = term
            else:
                out_ref[cols, :] = term.astype(BF16)
    mover.start(out_ref, out_hbm).wait()


def outer(a, b, step):
    rows, width = a.shape
    return pl.pallas_call(
        functools.partial(outer_kernel, step=step),
        in_specs=[HBM] * 2,
        out_specs=HBM,
        out_shape=pltpu.HBM((width, DH), BF16),
        scratch_shapes=[
            pltpu.VMEM((rows, width), BF16),
            pltpu.VMEM((rows, width), BF16),
            pltpu.VMEM((width, DH), F32),
            pltpu.VMEM((width, DH), BF16),
            pltpu.SemaphoreType.DMA((2 * rows // step + 1,)),
        ],
        compiler_params=params(VMEM_MOST),
        name="outer",
    )(far(a), far(b))


def scan_kernel(x_ref, out_ref, *, backward):
    count = x_ref.shape[0]
    total = jnp.zeros(x_ref.shape[1:], F32)
    for lap in range(count):
        i = count - 1 - lap if backward else lap
        out_ref[i] = total.astype(BF16)
        total = total + x_ref[i].astype(F32)


def scan(x, backward):
    return pl.pallas_call(
        functools.partial(scan_kernel, backward=backward),
        out_shape=jax.ShapeDtypeStruct(x.shape, BF16),
        cost_estimate=pl.CostEstimate(flops=SCAN_COST, bytes_accessed=SCAN_COST // 300, transcendentals=0),
        compiler_params=params(),
        name="suffix" if backward else "prefix",
    )(x)


def exchange(x, axis):
    return lax.all_to_all(x, axis, 0, 0)


def keep_lower(x):
    row = lax.broadcasted_iota(jnp.int32, x.shape, 0)
    col = lax.broadcasted_iota(jnp.int32, x.shape, 1)
    return jnp.where(row >= col, x, 0.0)


def keep_upper(x):
    row = lax.broadcasted_iota(jnp.int32, x.shape, 0)
    col = lax.broadcasted_iota(jnp.int32, x.shape, 1)
    return jnp.where(row <= col, x, 0.0)


def lower_parts(a, b):
    half = a.shape[0] // 2
    return (
        keep_lower(dot(a[:half], b[:half], NT)).astype(BF16),
        dot(a[half:], b[:half], NT).astype(BF16),
        keep_lower(dot(a[half:], b[half:], NT)).astype(BF16),
    )


def upper_parts(a, b):
    half = a.shape[0] // 2
    return (
        keep_upper(dot(a[:half], b[:half], NT)).astype(BF16),
        dot(a[:half], b[half:], NT).astype(BF16),
        keep_upper(dot(a[half:], b[half:], NT)).astype(BF16),
    )


def lower_apply(parts, c):
    top, low, last = parts
    half = top.shape[0]
    return dot(top, c[:half], NN), dot(low, c[:half], NN) + dot(last, c[half:], NN)


def upper_apply(parts, c):
    top, high, last = parts
    half = top.shape[0]
    return dot(top, c[:half], NN) + dot(high, c[half:], NN), dot(last, c[half:], NN)


def upper_turned(parts, c):
    top, high, last = parts
    half = top.shape[0]
    return dot(top, c[:half], TN), dot(high, c[:half], TN) + dot(last, c[half:], TN)


def put(ref, cols, pair):
    half = ref.shape[0] // 2
    ref[:half, cols] = pair[0].astype(ref.dtype)
    ref[half:, cols] = pair[1].astype(ref.dtype)


def within_kernel(q_hbm, k_hbm, v_hbm, out_hbm, q_ref, k_ref, v_ref, out_ref, sems, *, step):
    mover = Mover(sems)
    groups = groups_of(q_ref, step)
    pairs = ((q_hbm, q_ref), (k_hbm, k_ref), (v_hbm, v_ref))
    loads = [[mover.start(src.at[:, group], dst.at[:, group]) for src, dst in pairs] for group in groups]
    stores = []
    for i, group in enumerate(groups):
        for copy in loads[i]:
            copy.wait()
        spans = heads_of(q_ref)[i * step // DH : (i + 1) * step // DH]
        parts = [lower_parts(q_ref[:, cols], k_ref[:, cols]) for cols in spans]
        for cols, part in zip(spans, parts):
            put(out_ref, cols, lower_apply(part, v_ref[:, cols]))
        stores.append(mover.start(out_ref.at[:, group], out_hbm.at[:, group]))
    for copy in stores:
        copy.wait()


def within(q, k, v, step):
    return pl.pallas_call(
        functools.partial(within_kernel, step=step),
        in_specs=[HBM] * 3,
        out_specs=HBM,
        out_shape=pltpu.HBM(q.shape, F32),
        scratch_shapes=[pltpu.VMEM(q.shape, BF16)] * 3 + [pltpu.VMEM(q.shape, F32), pltpu.SemaphoreType.DMA((4 * q.shape[1] // step,))],
        compiler_params=params(VMEM_MOST),
        name="within",
    )(far(q), far(k), far(v))


def attend_kernel(a_ref, q_ref, s_ref, cot_ref, gain_ref, att_ref, stat_ref, sum_ref):
    chunks = chunks_of(q_ref, DH)
    for i, span in enumerate(chunks):
        sq = jnp.zeros((DH, DH), F32)
        cr = jnp.zeros((DH, DH), F32)
        for cols in heads_of(q_ref):
            att = a_ref[span, cols] + dot(q_ref[span, cols], s_ref[cols, :], NN)
            att_ref[span, cols] = att
            scaled = cot_ref[span, cols].astype(F32) * gain_ref[:, cols].astype(F32)
            sq += att * att
            cr += scaled * att
        sum_ref[i] = sq
        sum_ref[len(chunks) + i] = cr
    lines = [jnp.sum(sum_ref[i].T, axis=0, keepdims=True) for i in range(sum_ref.shape[0])]
    lines = jnp.concatenate(lines, axis=0)
    for copy in range(stat_ref.shape[0]):
        stat_ref[copy] = lines


def attend(a, q, s, cot, gain, copies):
    rows, width = q.shape
    return pl.pallas_call(
        attend_kernel,
        out_shape=[
            jax.ShapeDtypeStruct((rows, width), F32),
            jax.ShapeDtypeStruct((copies, 2 * rows // DH, DH), F32),
        ],
        scratch_shapes=[pltpu.VMEM((2 * rows // DH, DH, DH), F32)],
        compiler_params=params(),
        name="attend",
    )(a, q, s, cot, gain)


def grad_kernel(
    att_ref, cot_ref, gain_ref, stat_ref, q_ref, g_hbm, lg_hbm, n_hbm, g_ref, lg_ref, n_ref, sems, *, total
):
    mover = Mover(sems)
    rows = att_ref.shape[0]
    blocks = rows // DH
    stats = jnp.sum(stat_ref[...], axis=0) / total
    inv = lax.rsqrt(stats[:blocks] + 1e-06)
    pull = inv**3 * stats[blocks:]
    stores = []
    for i, span in enumerate(chunks_of(att_ref, DH)):
        inv_tile = jnp.broadcast_to(inv[i : i + 1], (DH, DH)).T
        pull_tile = jnp.broadcast_to(pull[i : i + 1], (DH, DH)).T
        for cols in heads_of(q_ref):
            gain = gain_ref[:, cols].astype(F32)
            att = att_ref[span, cols]
            scaled = cot_ref[span, cols].astype(F32) * gain
            g_ref[span, cols] = (inv_tile * scaled - att * pull_tile).astype(BF16)
            n_ref[span, cols] = (att * inv_tile * gain).astype(BF16)
        stores.append(mover.start(g_ref.at[span], g_hbm.at[span]))
        stores.append(mover.start(n_ref.at[span], n_hbm.at[span]))
    for cols in heads_of(q_ref):
        lg_ref[cols, :] = dot(q_ref[:, cols], g_ref[:, cols], TN).astype(BF16)
    stores.append(mover.start(lg_ref, lg_hbm))
    for copy in stores:
        copy.wait()


def grad(att, cot, gain, stats, q, total):
    rows, width = q.shape
    shapes = [(rows, width), (width, DH), (rows, width)]
    return pl.pallas_call(
        functools.partial(grad_kernel, total=total),
        out_specs=[HBM] * 3,
        out_shape=[pltpu.HBM(shape, BF16) for shape in shapes],
        scratch_shapes=[pltpu.VMEM(shape, BF16) for shape in shapes]
        + [pltpu.SemaphoreType.DMA((2 * rows // DH + 1,))],
        compiler_params=params(),
        name="grad",
    )(att, cot, gain, stats, q)


def side_kernel(q_hbm, k_hbm, v_hbm, g_hbm, s_hbm, *refs, step):
    gq_hbm, gk_hbm, gv_hbm, q_ref, k_ref, v_ref, g_ref, s_ref, gq_ref, gk_ref, gv_ref, sems = refs
    mover = Mover(sems)
    half = q_ref.shape[0] // 2
    groups = groups_of(q_ref, step)
    here = step // DH
    s_in = mover.start(s_hbm, s_ref)
    pairs = ((g_hbm, g_ref), (v_hbm, v_ref), (k_hbm, k_ref), (q_hbm, q_ref))
    loads = [[mover.start(src.at[:, group], dst.at[:, group]) for src, dst in pairs] for group in groups]
    stores = []
    s_in.wait()
    for i, group in enumerate(groups):
        for copy in loads[i]:
            copy.wait()
        spans = heads_of(q_ref)[i * here : (i + 1) * here]
        for cols in spans:
            q, k, v, g = q_ref[:, cols], k_ref[:, cols], v_ref[:, cols], g_ref[:, cols]
            pull = upper_parts(v, g)
            attn = upper_parts(k, q)
            rest = dot(g, s_ref[cols, :], NT)
            put(gk_ref, cols, upper_apply(pull, q))
            one, two = upper_turned(pull, k)
            put(gq_ref, cols, (one + rest[:half], two + rest[half:]))
            put(gv_ref, cols, upper_apply(attn, g))
        for src, dst in ((gk_ref, gk_hbm), (gv_ref, gv_hbm), (gq_ref, gq_hbm)):
            stores.append(mover.start(src.at[:, group], dst.at[:, group]))
    for copy in stores:
        copy.wait()


def side(q, k, v, g, s, step):
    outs = [pltpu.HBM(q.shape, kind) for kind in (BF16, PART, PART)]
    ins = (q, k, v, g, s)
    return pl.pallas_call(
        functools.partial(side_kernel, step=step),
        in_specs=[HBM] * len(ins),
        out_specs=[HBM] * len(outs),
        out_shape=outs,
        scratch_shapes=[pltpu.VMEM(x.shape, x.dtype) for x in (*ins, *outs)]
        + [pltpu.SemaphoreType.DMA((1 + 7 * q.shape[1] // step,))],
        compiler_params=params(VMEM_MOST),
        name="side",
    )(*[far(x) for x in ins])


def last_kernel(gk_ref, gv_ref, k_ref, v_ref, s_ref, outk_hbm, outv_hbm, outk_ref, outv_ref, sems, *, step):
    mover = Mover(sems)
    stores = []
    for group in groups_of(k_ref, step):
        for cols in heads_of(k_ref)[group.start // DH : group.stop // DH]:
            s = s_ref[cols, :]
            outk_ref[:, cols] = (gk_ref[:, cols] + dot(v_ref[:, cols], s, NT)).astype(BF16)
            outv_ref[:, cols] = (gv_ref[:, cols] + dot(k_ref[:, cols], s, NN)).astype(BF16)
        stores.append(mover.start(outk_ref.at[:, group], outk_hbm.at[:, group]))
        stores.append(mover.start(outv_ref.at[:, group], outv_hbm.at[:, group]))
    for copy in stores:
        copy.wait()


def last(gk, gv, k, v, s, step):
    rows, width = k.shape
    return pl.pallas_call(
        functools.partial(last_kernel, step=step),
        out_specs=[HBM] * 2,
        out_shape=[pltpu.HBM((rows, width), BF16)] * 2,
        scratch_shapes=[pltpu.VMEM((rows, width), BF16)] * 2 + [pltpu.SemaphoreType.DMA((2 * width // step,))],
        compiler_params=params(),
        name="last",
    )(gk, gv, k, v, s)


def body(queries, keys, values, gain, cotangent):
    rows, width = queries.shape
    count, heads = lax.axis_size("ctx"), lax.axis_size("head")
    gain = gain.reshape(1, width)
    parts = (count, width // count, DH)

    local = exchange(outer(keys, values, 128).reshape(parts), "ctx")
    a = within(queries, keys, values, 256)
    local, a, gain = lax.optimization_barrier((local, a, gain))
    state = exchange(scan(local, False), "ctx").reshape(width, DH)

    att, stats = attend(a, queries, state, cotangent, gain, heads)
    stats = exchange(stats, "head")
    g, local, normed = grad(att, cotangent, gain, stats, queries, width * heads)

    local = exchange(local.reshape(parts), "ctx")
    sides = side(queries, keys, values, g, state, 256)
    local, grad_q, gk, gv = lax.optimization_barrier((local, *sides))
    later = exchange(scan(local, True), "ctx").reshape(width, DH)
    grad_k, grad_v = last(gk, gv, keys, values, later, 256)
    return normed, grad_q, grad_k, grad_v


def solution(mesh):
    return jax.shard_map(
        body,
        mesh=mesh,
        in_specs=(
            P("ctx", "head"),
            P("ctx", "head"),
            P("ctx", "head"),
            P("head"),
            P("ctx", "head"),
        ),
        out_specs=(P("ctx", "head"), P("ctx", "head"), P("ctx", "head"), P("ctx", "head")),
        check_vma=False,
    )
```

```python
import functools

import jax
import jax.numpy as jnp
from jax import lax
from jax.experimental import pallas as pl
from jax.experimental.pallas import tpu as pltpu
from jax.sharding import PartitionSpec as P

DH = 128
F32 = jnp.float32
BF16 = jnp.bfloat16
PART = F32
FIRST = 18
SCAN_COST = 10_000_000_000
VMEM_LIMIT = 16 * 1024 * 1024
VMEM_MOST = 60 * 1024 * 1024
VMEM = pl.BlockSpec(memory_space=pltpu.VMEM)


def far(x):
    return pltpu.with_memory_space_constraint(x, pltpu.HBM)


NT = (((1,), (1,)), ((), ()))
NN = (((1,), (0,)), ((), ()))
TN = (((0,), (0,)), ((), ()))


def dot(a, b, dims):
    return lax.dot_general(a, b, dims, preferred_element_type=F32)


def params(limit=VMEM_LIMIT):
    return pltpu.CompilerParams(vmem_limit_bytes=limit)


def heads_of(ref):
    return [slice(c, c + DH) for c in range(0, ref.shape[1], DH)]


HBM = pl.BlockSpec(memory_space=pltpu.HBM)


class Mover:
    def __init__(self, sems):
        self.sems = sems
        self.used = 0

    def start(self, src, dst):
        copy = pltpu.make_async_copy(src, dst, self.sems.at[self.used])
        self.used += 1
        copy.start()
        return copy


def chunks_of(ref, step):
    return [slice(r, r + step) for r in range(0, ref.shape[0], step)]


def groups_of(ref, step):
    return [slice(c, c + step) for c in range(0, ref.shape[1], step)]


def outer_kernel(a_hbm, b_hbm, out_hbm, a_ref, b_ref, acc_ref, out_ref, sems, *, step):
    mover = Mover(sems)
    chunks = chunks_of(a_ref, step)
    loads = [
        (mover.start(a_hbm.at[rows], a_ref.at[rows]), mover.start(b_hbm.at[rows], b_ref.at[rows])) for rows in chunks
    ]
    stores = []
    for i, rows in enumerate(chunks):
        for copy in loads[i]:
            copy.wait()
        for h, cols in enumerate(heads_of(a_ref)):
            term = dot(a_ref[rows, cols], b_ref[rows, cols], TN)
            if i > 0:
                term = acc_ref[cols, :] + term
            if i < len(chunks) - 1:
                acc_ref[cols, :] = term
                continue
            out_ref[cols, :] = term.astype(BF16)
            if h % 4 == 3:
                four = slice(cols.stop - 4 * DH, cols.stop)
                stores.append(mover.start(out_ref.at[four], out_hbm.at[four]))
    for copy in stores:
        copy.wait()


def outer(a, b, step):
    rows, width = a.shape
    return pl.pallas_call(
        functools.partial(outer_kernel, step=step),
        in_specs=[HBM] * 2,
        out_specs=HBM,
        out_shape=pltpu.HBM((width, DH), BF16),
        scratch_shapes=[
            pltpu.VMEM((rows, width), BF16),
            pltpu.VMEM((rows, width), BF16),
            pltpu.VMEM((width, DH), F32),
            pltpu.VMEM((width, DH), BF16),
            pltpu.SemaphoreType.DMA((2 * rows // step + width // DH // 4,)),
        ],
        compiler_params=params(VMEM_MOST),
        name="outer",
    )(far(a), far(b))


def ring(count, first):
    return [(first + i) % count for i in range(count)]


def scan_kernel(x_ref, out_ref, *, backward):
    count = x_ref.shape[0]
    total = jnp.zeros(x_ref.shape[1:], F32)
    place = {block: i for i, block in enumerate(ring(count, FIRST))}
    for lap in range(count):
        i = place[count - 1 - lap if backward else lap]
        out_ref[i] = total.astype(BF16)
        total = total + x_ref[i].astype(F32)


def scan(x, backward):
    return pl.pallas_call(
        functools.partial(scan_kernel, backward=backward),
        out_shape=jax.ShapeDtypeStruct(x.shape, BF16),
        cost_estimate=pl.CostEstimate(flops=SCAN_COST, bytes_accessed=SCAN_COST // 300, transcendentals=0),
        compiler_params=params(),
        name="suffix" if backward else "prefix",
    )(x)


def exchange(x, axis):
    return lax.all_to_all(x, axis, 0, 0, axis_index_groups=[ring(x.shape[0], FIRST)])


def gathered(x, axis):
    count = lax.axis_size(axis)
    pair = x + lax.ppermute(x, axis, [(i, i ^ 1) for i in range(count)])
    steps = range(2, count, 2)
    return [pair, *(lax.ppermute(pair, axis, [(i, (i + d) % count) for i in range(count)]) for d in steps)]


def keep_lower(x):
    row = lax.broadcasted_iota(jnp.int32, x.shape, 0)
    col = lax.broadcasted_iota(jnp.int32, x.shape, 1)
    return jnp.where(row >= col, x, 0.0)


def keep_upper(x):
    row = lax.broadcasted_iota(jnp.int32, x.shape, 0)
    col = lax.broadcasted_iota(jnp.int32, x.shape, 1)
    return jnp.where(row <= col, x, 0.0)


def lower_parts(a, b):
    half = a.shape[0] // 2
    return (
        keep_lower(dot(a[:half], b[:half], NT)).astype(BF16),
        dot(a[half:], b[:half], NT).astype(BF16),
        keep_lower(dot(a[half:], b[half:], NT)).astype(BF16),
    )


def upper_parts(a, b):
    half = a.shape[0] // 2
    return (
        keep_upper(dot(a[:half], b[:half], NT)).astype(BF16),
        dot(a[:half], b[half:], NT).astype(BF16),
        keep_upper(dot(a[half:], b[half:], NT)).astype(BF16),
    )


def lower_apply(parts, c):
    top, low, last = parts
    half = top.shape[0]
    return dot(top, c[:half], NN), dot(low, c[:half], NN) + dot(last, c[half:], NN)


def upper_apply(parts, c):
    top, high, last = parts
    half = top.shape[0]
    return dot(top, c[:half], NN) + dot(high, c[half:], NN), dot(last, c[half:], NN)


def upper_turned(parts, c):
    top, high, last = parts
    half = top.shape[0]
    return dot(top, c[:half], TN), dot(high, c[:half], TN) + dot(last, c[half:], TN)


def put(ref, cols, pair):
    half = ref.shape[0] // 2
    ref[:half, cols] = pair[0].astype(ref.dtype)
    ref[half:, cols] = pair[1].astype(ref.dtype)


def within_kernel(q_hbm, k_hbm, v_hbm, out_hbm, q_ref, k_ref, v_ref, out_ref, sems, *, step):
    mover = Mover(sems)
    groups = groups_of(q_ref, step)
    pairs = ((q_hbm, q_ref), (k_hbm, k_ref), (v_hbm, v_ref))
    loads = [[mover.start(src.at[:, group], dst.at[:, group]) for src, dst in pairs] for group in groups]
    stores = []
    for i, group in enumerate(groups):
        for copy in loads[i]:
            copy.wait()
        spans = heads_of(q_ref)[i * step // DH : (i + 1) * step // DH]
        parts = [lower_parts(q_ref[:, cols], k_ref[:, cols]) for cols in spans]
        for cols, part in zip(spans, parts):
            put(out_ref, cols, lower_apply(part, v_ref[:, cols]))
        stores.append(mover.start(out_ref.at[:, group], out_hbm.at[:, group]))
    for copy in stores:
        copy.wait()


def within(q, k, v, step):
    return pl.pallas_call(
        functools.partial(within_kernel, step=step),
        in_specs=[HBM] * 3,
        out_specs=HBM,
        out_shape=pltpu.HBM(q.shape, F32),
        scratch_shapes=[pltpu.VMEM(q.shape, BF16)] * 3 + [pltpu.VMEM(q.shape, F32), pltpu.SemaphoreType.DMA((4 * q.shape[1] // step,))],
        compiler_params=params(VMEM_MOST),
        name="within",
    )(far(q), far(k), far(v))


def side_by_side(one, two):
    return jnp.concatenate(
        [
            jnp.concatenate([one, jnp.zeros_like(two)], axis=1),
            jnp.concatenate([jnp.zeros_like(one), two], axis=1),
        ],
        axis=0,
    )


def attend_kernel(a_ref, q_ref, s_ref, cot_ref, gain_ref, att_ref, stat_ref, sq_ref, cr_ref):
    for i, pair in enumerate(groups_of(q_ref, 2 * DH)):
        s = side_by_side(s_ref[pair.start : pair.start + DH, :], s_ref[pair.start + DH : pair.stop, :])
        att = a_ref[:, pair] + dot(q_ref[:, pair], s, NN)
        att_ref[:, pair] = att
        scaled = cot_ref[:, pair].astype(F32) * gain_ref[:, pair].astype(F32)
        for ref, term in ((sq_ref, att * att), (cr_ref, scaled * att)):
            term = term[:, :DH] + term[:, DH:]
            ref[...] = term if i == 0 else ref[...] + term
    chunks = chunks_of(q_ref, DH)
    lines = [jnp.sum(ref[span, :].T, axis=0, keepdims=True) for ref in (sq_ref, cr_ref) for span in chunks]
    stat_ref[...] = jnp.concatenate(lines, axis=0)


def attend(a, q, s, cot, gain):
    rows, width = q.shape
    return pl.pallas_call(
        attend_kernel,
        out_shape=[
            jax.ShapeDtypeStruct((rows, width), F32),
            jax.ShapeDtypeStruct((2 * rows // DH, DH), F32),
        ],
        scratch_shapes=[pltpu.VMEM((rows, DH), F32)] * 2,
        compiler_params=params(),
        name="attend",
    )(a, q, s, cot, gain)


def grad_kernel(
    att_ref, cot_ref, gain_ref, q_ref, s0_ref, s1_ref, s2_ref, s3_ref, g_hbm, lg_hbm, n_hbm, g_ref, lg_ref, n_ref, sems, *, total
):
    mover = Mover(sems)
    rows = att_ref.shape[0]
    blocks = rows // DH
    stats = ((s0_ref[...] + s1_ref[...]) + (s2_ref[...] + s3_ref[...])) / total
    inv = lax.rsqrt(stats[:blocks] + 1e-06)
    pull = inv**3 * stats[blocks:]
    stores = []
    for i, span in enumerate(chunks_of(att_ref, DH)):
        inv_tile = jnp.broadcast_to(inv[i : i + 1], (DH, DH)).T
        pull_tile = jnp.broadcast_to(pull[i : i + 1], (DH, DH)).T
        for cols in heads_of(q_ref):
            gain = gain_ref[:, cols].astype(F32)
            att = att_ref[span, cols]
            scaled = cot_ref[span, cols].astype(F32) * gain
            g_ref[span, cols] = (inv_tile * scaled - att * pull_tile).astype(BF16)
            n_ref[span, cols] = (att * inv_tile * gain).astype(BF16)
        stores.append(mover.start(g_ref.at[span], g_hbm.at[span]))
        stores.append(mover.start(n_ref.at[span], n_hbm.at[span]))
    for cols in heads_of(q_ref):
        lg_ref[cols, :] = dot(q_ref[:, cols], g_ref[:, cols], TN).astype(BF16)
    stores.append(mover.start(lg_ref, lg_hbm))
    for copy in stores:
        copy.wait()


def grad(att, cot, gain, stats, q, total):
    rows, width = q.shape
    shapes = [(rows, width), (width, DH), (rows, width)]
    return pl.pallas_call(
        functools.partial(grad_kernel, total=total),
        out_specs=[HBM] * 3,
        out_shape=[pltpu.HBM(shape, BF16) for shape in shapes],
        scratch_shapes=[pltpu.VMEM(shape, BF16) for shape in shapes]
        + [pltpu.SemaphoreType.DMA((2 * rows // DH + 1,))],
        compiler_params=params(),
        name="grad",
    )(att, cot, gain, q, *stats)


def side_kernel(q_hbm, k_hbm, v_hbm, g_hbm, s_hbm, *refs, step):
    gq_hbm, gk_hbm, gv_hbm, q_ref, k_ref, v_ref, g_ref, s_ref, gq_ref, gk_ref, gv_ref, sems = refs
    mover = Mover(sems)
    half = q_ref.shape[0] // 2
    groups = groups_of(q_ref, step)
    many = step // DH
    s_in = mover.start(s_hbm, s_ref)
    pairs = ((g_hbm, g_ref), (v_hbm, v_ref), (k_hbm, k_ref), (q_hbm, q_ref))
    loads = [[mover.start(src.at[:, group], dst.at[:, group]) for src, dst in pairs] for group in groups]
    stores = []
    s_in.wait()
    for i, group in enumerate(groups):
        for copy in loads[i]:
            copy.wait()
        spans = heads_of(q_ref)[i * many : (i + 1) * many]
        for j, cols in enumerate(spans):
            if j % 2 == 0:
                span = slice(cols.start, cols.start + 2 * DH)
                s = side_by_side(s_ref[cols, :].T, s_ref[cols.stop : span.stop, :].T)
                rest = dot(g_ref[:, span], s, NN)
            here = slice(j % 2 * DH, (j % 2 + 1) * DH)
            q, k, v, g = q_ref[:, cols], k_ref[:, cols], v_ref[:, cols], g_ref[:, cols]
            pull = upper_parts(v, g)
            attn = upper_parts(k, q)
            put(gk_ref, cols, upper_apply(pull, q))
            one, two = upper_turned(pull, k)
            put(gq_ref, cols, (one + rest[:half, here], two + rest[half:, here]))
            put(gv_ref, cols, upper_apply(attn, g))
        for src, dst in ((gk_ref, gk_hbm), (gv_ref, gv_hbm), (gq_ref, gq_hbm)):
            stores.append(mover.start(src.at[:, group], dst.at[:, group]))
    for copy in stores:
        copy.wait()


def side(q, k, v, g, s, step):
    outs = [pltpu.HBM(q.shape, kind) for kind in (BF16, PART, PART)]
    ins = (q, k, v, g, s)
    return pl.pallas_call(
        functools.partial(side_kernel, step=step),
        in_specs=[HBM] * len(ins),
        out_specs=[HBM] * len(outs),
        out_shape=outs,
        scratch_shapes=[pltpu.VMEM(x.shape, x.dtype) for x in (*ins, *outs)]
        + [pltpu.SemaphoreType.DMA((1 + 7 * q.shape[1] // step,))],
        compiler_params=params(VMEM_MOST),
        name="side",
    )(*[far(x) for x in ins])


def last_kernel(gk_ref, gv_ref, k_ref, v_ref, s_ref, outk_hbm, outv_hbm, outk_ref, outv_ref, sems, *, step):
    mover = Mover(sems)
    stores = []
    for group in groups_of(k_ref, step):
        for cols in heads_of(k_ref)[group.start // DH : group.stop // DH]:
            s = s_ref[cols, :]
            both = dot(jnp.concatenate([v_ref[:, cols], k_ref[:, cols]], axis=1), side_by_side(s.T, s), NN)
            outk_ref[:, cols] = (gk_ref[:, cols] + both[:, :DH]).astype(BF16)
            outv_ref[:, cols] = (gv_ref[:, cols] + both[:, DH:]).astype(BF16)
        stores.append(mover.start(outk_ref.at[:, group], outk_hbm.at[:, group]))
        stores.append(mover.start(outv_ref.at[:, group], outv_hbm.at[:, group]))
    for copy in stores:
        copy.wait()


def last(gk, gv, k, v, s, step):
    rows, width = k.shape
    return pl.pallas_call(
        functools.partial(last_kernel, step=step),
        out_specs=[HBM] * 2,
        out_shape=[pltpu.HBM((rows, width), BF16)] * 2,
        scratch_shapes=[pltpu.VMEM((rows, width), BF16)] * 2 + [pltpu.SemaphoreType.DMA((2 * width // step,))],
        compiler_params=params(),
        name="last",
    )(gk, gv, k, v, s)


def body(queries, keys, values, gain, cotangent):
    rows, width = queries.shape
    count, heads = lax.axis_size("ctx"), lax.axis_size("head")
    gain = gain.reshape(1, width)
    parts = (count, width // count, DH)

    local = exchange(outer(keys, values, 128).reshape(parts), "ctx")
    a = within(queries, keys, values, 256)
    local, a, gain = lax.optimization_barrier((local, a, gain))
    state = exchange(scan(local, False), "ctx").reshape(width, DH)

    att, stats = attend(a, queries, state, cotangent, gain)
    stats = gathered(stats, "head")
    g, local, normed = grad(att, cotangent, gain, stats, queries, width * heads)

    local = exchange(local.reshape(parts), "ctx")
    sides = side(queries, keys, values, g, state, 256)
    local, grad_q, gk, gv = lax.optimization_barrier((local, *sides))
    later = exchange(scan(local, True), "ctx").reshape(width, DH)
    grad_k, grad_v = last(gk, gv, keys, values, later, 256)
    return normed, grad_q, grad_k, grad_v


def solution(mesh):
    return jax.shard_map(
        body,
        mesh=mesh,
        in_specs=(
            P("ctx", "head"),
            P("ctx", "head"),
            P("ctx", "head"),
            P("head"),
            P("ctx", "head"),
        ),
        out_specs=(P("ctx", "head"), P("ctx", "head"), P("ctx", "head"), P("ctx", "head")),
        check_vma=False,
    )
```

```python
import functools

import jax
import jax.numpy as jnp
from jax import lax
from jax.experimental import pallas as pl
from jax.experimental.pallas import tpu as pltpu
from jax.sharding import PartitionSpec as P

DH = 128
F32 = jnp.float32
BF16 = jnp.bfloat16
PART = F32
FIRST = 18
SCAN_COST = 10_000_000_000
VMEM_LIMIT = 16 * 1024 * 1024
VMEM_MOST = 60 * 1024 * 1024
SIDE_VMEM = 24 * 1024 * 1024
VMEM = pl.BlockSpec(memory_space=pltpu.VMEM)


def far(x):
    return pltpu.with_memory_space_constraint(x, pltpu.HBM)


NT = (((1,), (1,)), ((), ()))
NN = (((1,), (0,)), ((), ()))
TN = (((0,), (0,)), ((), ()))


def dot(a, b, dims):
    return lax.dot_general(a, b, dims, preferred_element_type=F32)


def params(limit=VMEM_LIMIT):
    return pltpu.CompilerParams(vmem_limit_bytes=limit)


def heads_of(ref):
    return [slice(c, c + DH) for c in range(0, ref.shape[1], DH)]


HBM = pl.BlockSpec(memory_space=pltpu.HBM)


class Mover:
    def __init__(self, sems):
        self.sems = sems
        self.used = 0

    def start(self, src, dst):
        copy = pltpu.make_async_copy(src, dst, self.sems.at[self.used])
        self.used += 1
        copy.start()
        return copy


def chunks_of(ref, step):
    return [slice(r, r + step) for r in range(0, ref.shape[0], step)]


def groups_of(ref, step):
    return [slice(c, c + step) for c in range(0, ref.shape[1], step)]


def outer_kernel(a_hbm, b_hbm, out_hbm, a_ref, b_ref, acc_ref, out_ref, sems, *, step):
    mover = Mover(sems)
    chunks = chunks_of(a_ref, step)
    loads = [
        (mover.start(a_hbm.at[rows], a_ref.at[rows]), mover.start(b_hbm.at[rows], b_ref.at[rows])) for rows in chunks
    ]
    stores = []
    for i, rows in enumerate(chunks):
        for copy in loads[i]:
            copy.wait()
        for h, cols in enumerate(heads_of(a_ref)):
            term = dot(a_ref[rows, cols], b_ref[rows, cols], TN)
            if i > 0:
                term = acc_ref[cols, :] + term
            if i < len(chunks) - 1:
                acc_ref[cols, :] = term
                continue
            out_ref[cols, :] = term.astype(BF16)
            if h % 4 == 3:
                four = slice(cols.stop - 4 * DH, cols.stop)
                stores.append(mover.start(out_ref.at[four], out_hbm.at[four]))
    for copy in stores:
        copy.wait()


def outer(a, b, step):
    rows, width = a.shape
    return pl.pallas_call(
        functools.partial(outer_kernel, step=step),
        in_specs=[HBM] * 2,
        out_specs=HBM,
        out_shape=pltpu.HBM((width, DH), BF16),
        scratch_shapes=[
            pltpu.VMEM((rows, width), BF16),
            pltpu.VMEM((rows, width), BF16),
            pltpu.VMEM((width, DH), F32),
            pltpu.VMEM((width, DH), BF16),
            pltpu.SemaphoreType.DMA((2 * rows // step + width // DH // 4,)),
        ],
        compiler_params=params(VMEM_MOST),
        name="outer",
    )(far(a), far(b))


def ring(count, first):
    return [(first + i) % count for i in range(count)]


def scan_kernel(x_ref, out_ref, *, backward):
    count = x_ref.shape[0]
    total = jnp.zeros(x_ref.shape[1:], F32)
    place = {block: i for i, block in enumerate(ring(count, FIRST))}
    for lap in range(count):
        i = place[count - 1 - lap if backward else lap]
        out_ref[i] = total.astype(BF16)
        total = total + x_ref[i].astype(F32)


def scan(x, backward):
    return pl.pallas_call(
        functools.partial(scan_kernel, backward=backward),
        out_shape=jax.ShapeDtypeStruct(x.shape, BF16),
        cost_estimate=pl.CostEstimate(flops=SCAN_COST, bytes_accessed=SCAN_COST // 300, transcendentals=0),
        compiler_params=params(),
        name="suffix" if backward else "prefix",
    )(x)


def exchange(x, axis):
    return lax.all_to_all(x, axis, 0, 0, axis_index_groups=[ring(x.shape[0], FIRST)])


def gathered(x, axis):
    count = lax.axis_size(axis)
    pair = x + lax.ppermute(x, axis, [(i, i ^ 1) for i in range(count)])
    steps = range(2, count, 2)
    return [pair, *(lax.ppermute(pair, axis, [(i, (i + d) % count) for i in range(count)]) for d in steps)]


def keep_lower(x):
    row = lax.broadcasted_iota(jnp.int32, x.shape, 0)
    col = lax.broadcasted_iota(jnp.int32, x.shape, 1)
    return jnp.where(row >= col, x, 0.0)


def keep_upper(x):
    row = lax.broadcasted_iota(jnp.int32, x.shape, 0)
    col = lax.broadcasted_iota(jnp.int32, x.shape, 1)
    return jnp.where(row <= col, x, 0.0)


def lower_parts(a, b):
    half = a.shape[0] // 2
    return (
        keep_lower(dot(a[:half], b[:half], NT)).astype(BF16),
        dot(a[half:], b[:half], NT).astype(BF16),
        keep_lower(dot(a[half:], b[half:], NT)).astype(BF16),
    )


def upper_parts(a, b):
    half = a.shape[0] // 2
    return (
        keep_upper(dot(a[:half], b[:half], NT)).astype(BF16),
        dot(a[:half], b[half:], NT).astype(BF16),
        keep_upper(dot(a[half:], b[half:], NT)).astype(BF16),
    )


def lower_apply(parts, c):
    top, low, last = parts
    half = top.shape[0]
    return dot(top, c[:half], NN), dot(low, c[:half], NN) + dot(last, c[half:], NN)


def upper_apply(parts, c):
    top, high, last = parts
    half = top.shape[0]
    return dot(top, c[:half], NN) + dot(high, c[half:], NN), dot(last, c[half:], NN)


def upper_turned(parts, c):
    top, high, last = parts
    half = top.shape[0]
    return dot(top, c[:half], TN), dot(high, c[:half], TN) + dot(last, c[half:], TN)


def put(ref, cols, pair):
    half = ref.shape[0] // 2
    ref[:half, cols] = pair[0].astype(ref.dtype)
    ref[half:, cols] = pair[1].astype(ref.dtype)


def within_kernel(q_hbm, k_hbm, v_hbm, out_hbm, q_ref, k_ref, v_ref, out_ref, sems, *, step):
    mover = Mover(sems)
    groups = groups_of(q_ref, step)
    pairs = ((q_hbm, q_ref), (k_hbm, k_ref), (v_hbm, v_ref))
    loads = [[mover.start(src.at[:, group], dst.at[:, group]) for src, dst in pairs] for group in groups]
    stores = []
    for i, group in enumerate(groups):
        for copy in loads[i]:
            copy.wait()
        spans = heads_of(q_ref)[i * step // DH : (i + 1) * step // DH]
        parts = [lower_parts(q_ref[:, cols], k_ref[:, cols]) for cols in spans]
        for cols, part in zip(spans, parts):
            put(out_ref, cols, lower_apply(part, v_ref[:, cols]))
        stores.append(mover.start(out_ref.at[:, group], out_hbm.at[:, group]))
    for copy in stores:
        copy.wait()


def within(q, k, v, step):
    return pl.pallas_call(
        functools.partial(within_kernel, step=step),
        in_specs=[HBM] * 3,
        out_specs=HBM,
        out_shape=pltpu.HBM(q.shape, F32),
        scratch_shapes=[pltpu.VMEM(q.shape, BF16)] * 3 + [pltpu.VMEM(q.shape, F32), pltpu.SemaphoreType.DMA((4 * q.shape[1] // step,))],
        compiler_params=params(VMEM_MOST),
        name="within",
    )(far(q), far(k), far(v))


def side_by_side(one, two):
    return jnp.concatenate(
        [
            jnp.concatenate([one, jnp.zeros_like(two)], axis=1),
            jnp.concatenate([jnp.zeros_like(one), two], axis=1),
        ],
        axis=0,
    )


def attend_kernel(a_ref, q_ref, s_ref, cot_ref, gain_ref, att_ref, stat_ref, sq_ref, cr_ref):
    for i, pair in enumerate(groups_of(q_ref, 2 * DH)):
        s = side_by_side(s_ref[pair.start : pair.start + DH, :], s_ref[pair.start + DH : pair.stop, :])
        att = a_ref[:, pair] + dot(q_ref[:, pair], s, NN)
        att_ref[:, pair] = att
        scaled = cot_ref[:, pair].astype(F32) * gain_ref[:, pair].astype(F32)
        for ref, term in ((sq_ref, att * att), (cr_ref, scaled * att)):
            term = term[:, :DH] + term[:, DH:]
            ref[...] = term if i == 0 else ref[...] + term
    chunks = chunks_of(q_ref, DH)
    lines = [jnp.sum(ref[span, :].T, axis=0, keepdims=True) for ref in (sq_ref, cr_ref) for span in chunks]
    stat_ref[...] = jnp.concatenate(lines, axis=0)


def attend(a, q, s, cot, gain):
    rows, width = q.shape
    return pl.pallas_call(
        attend_kernel,
        out_shape=[
            jax.ShapeDtypeStruct((rows, width), F32),
            jax.ShapeDtypeStruct((2 * rows // DH, DH), F32),
        ],
        scratch_shapes=[pltpu.VMEM((rows, DH), F32)] * 2,
        compiler_params=params(),
        name="attend",
    )(a, q, s, cot, gain)


def grad_kernel(
    att_ref, cot_ref, gain_ref, q_ref, s0_ref, s1_ref, s2_ref, s3_ref, g_hbm, lg_hbm, n_hbm, g_ref, lg_ref, n_ref, sems, *, total
):
    mover = Mover(sems)
    rows = att_ref.shape[0]
    blocks = rows // DH
    stats = ((s0_ref[...] + s1_ref[...]) + (s2_ref[...] + s3_ref[...])) / total
    inv = lax.rsqrt(stats[:blocks] + 1e-06)
    pull = inv**3 * stats[blocks:]
    stores = []
    for i, span in enumerate(chunks_of(att_ref, DH)):
        inv_tile = jnp.broadcast_to(inv[i : i + 1], (DH, DH)).T
        pull_tile = jnp.broadcast_to(pull[i : i + 1], (DH, DH)).T
        for cols in heads_of(q_ref):
            gain = gain_ref[:, cols].astype(F32)
            att = att_ref[span, cols]
            scaled = cot_ref[span, cols].astype(F32) * gain
            g_ref[span, cols] = (inv_tile * scaled - att * pull_tile).astype(BF16)
            n_ref[span, cols] = (att * inv_tile * gain).astype(BF16)
        stores.append(mover.start(g_ref.at[span], g_hbm.at[span]))
        stores.append(mover.start(n_ref.at[span], n_hbm.at[span]))
    for cols in heads_of(q_ref):
        lg_ref[cols, :] = dot(q_ref[:, cols], g_ref[:, cols], TN).astype(BF16)
    stores.append(mover.start(lg_ref, lg_hbm))
    for copy in stores:
        copy.wait()


def grad(att, cot, gain, stats, q, total):
    rows, width = q.shape
    shapes = [(rows, width), (width, DH), (rows, width)]
    return pl.pallas_call(
        functools.partial(grad_kernel, total=total),
        out_specs=[HBM] * 3,
        out_shape=[pltpu.HBM(shape, BF16) for shape in shapes],
        scratch_shapes=[pltpu.VMEM(shape, BF16) for shape in shapes]
        + [pltpu.SemaphoreType.DMA((2 * rows // DH + 1,))],
        cost_estimate=pl.CostEstimate(flops=SCAN_COST, bytes_accessed=SCAN_COST // 300, transcendentals=0),
        compiler_params=params(),
        name="grad",
    )(att, cot, gain, q, *stats)


def side_kernel(q_ref, k_ref, v_hbm, g_hbm, s_hbm, *refs, sizes):
    gq_hbm, gk_hbm, gv_hbm, v_ref, g_ref, s_ref, gq_ref, gk_ref, gv_ref, sems = refs
    mover = Mover(sems)
    half = q_ref.shape[0] // 2
    groups = []
    for size in sizes:
        start = groups[-1].stop if groups else 0
        groups.append(slice(start, start + size * DH))
    s_in = mover.start(s_hbm, s_ref)
    pairs = ((g_hbm, g_ref), (v_hbm, v_ref))
    loads = [[mover.start(src.at[:, group], dst.at[:, group]) for src, dst in pairs] for group in groups]
    stores = []
    for i, group in enumerate(groups):
        spans = heads_of(q_ref)[group.start // DH : group.stop // DH]
        if i == 0:
            first = [upper_parts(k_ref[:, cols], q_ref[:, cols]) for cols in spans]
            s_in.wait()
        for copy in loads[i]:
            copy.wait()
        for j, cols in enumerate(spans):
            q, k, v, g = q_ref[:, cols], k_ref[:, cols], v_ref[:, cols], g_ref[:, cols]
            pull = upper_parts(v, g)
            attn = first[j] if i == 0 else upper_parts(k, q)
            rest = dot(g, s_ref[cols, :], NT)
            put(gk_ref, cols, upper_apply(pull, q))
            one, two = upper_turned(pull, k)
            put(gq_ref, cols, (one + rest[:half], two + rest[half:]))
            put(gv_ref, cols, upper_apply(attn, g))
        for src, dst in ((gk_ref, gk_hbm), (gv_ref, gv_hbm), (gq_ref, gq_hbm)):
            stores.append(mover.start(src.at[:, group], dst.at[:, group]))
    for copy in stores:
        copy.wait()


def side(q, k, v, g, s, sizes):
    outs = [pltpu.HBM(q.shape, kind) for kind in (BF16, PART, PART)]
    ins = (q, k, v, g, s)
    return pl.pallas_call(
        functools.partial(side_kernel, sizes=sizes),
        in_specs=[VMEM] * 2 + [HBM] * 3,
        out_specs=[HBM] * len(outs),
        out_shape=outs,
        scratch_shapes=[pltpu.VMEM(x.shape, x.dtype) for x in (*ins[2:], *outs)]
        + [pltpu.SemaphoreType.DMA((1 + 5 * len(sizes),))],
        compiler_params=params(SIDE_VMEM),
        name="side",
    )(q, k, *[far(x) for x in ins[2:]])


def last_kernel(gk_ref, gv_ref, k_ref, v_ref, s_ref, outk_hbm, outv_hbm, outk_ref, outv_ref, sems, *, step):
    mover = Mover(sems)
    stores = []
    for group in groups_of(k_ref, step):
        for cols in heads_of(k_ref)[group.start // DH : group.stop // DH]:
            s = s_ref[cols, :]
            both = dot(jnp.concatenate([v_ref[:, cols], k_ref[:, cols]], axis=1), side_by_side(s.T, s), NN)
            outk_ref[:, cols] = (gk_ref[:, cols] + both[:, :DH]).astype(BF16)
            outv_ref[:, cols] = (gv_ref[:, cols] + both[:, DH:]).astype(BF16)
        stores.append(mover.start(outk_ref.at[:, group], outk_hbm.at[:, group]))
        stores.append(mover.start(outv_ref.at[:, group], outv_hbm.at[:, group]))
    for copy in stores:
        copy.wait()


def last(gk, gv, k, v, s, step):
    rows, width = k.shape
    return pl.pallas_call(
        functools.partial(last_kernel, step=step),
        out_specs=[HBM] * 2,
        out_shape=[pltpu.HBM((rows, width), BF16)] * 2,
        scratch_shapes=[pltpu.VMEM((rows, width), BF16)] * 2 + [pltpu.SemaphoreType.DMA((2 * width // step,))],
        compiler_params=params(),
        name="last",
    )(gk, gv, k, v, s)


def body(queries, keys, values, gain, cotangent):
    rows, width = queries.shape
    count, heads = lax.axis_size("ctx"), lax.axis_size("head")
    gain = gain.reshape(1, width)
    parts = (count, width // count, DH)

    local = exchange(outer(keys, values, 128).reshape(parts), "ctx")
    a = within(queries, keys, values, 256)
    local, a, gain = lax.optimization_barrier((local, a, gain))
    state = exchange(scan(local, False), "ctx").reshape(width, DH)

    att, stats = attend(a, queries, state, cotangent, gain)
    stats = gathered(stats, "head")
    g, local, normed = grad(att, cotangent, gain, stats, queries, width * heads)

    local = exchange(local.reshape(parts), "ctx")
    sides = side(queries, keys, values, g, state, (2, 4, 2))
    local, grad_q, gk, gv = lax.optimization_barrier((local, *sides))
    later = exchange(scan(local, True), "ctx").reshape(width, DH)
    grad_k, grad_v = last(gk, gv, keys, values, later, 256)
    return normed, grad_q, grad_k, grad_v


def solution(mesh):
    return jax.shard_map(
        body,
        mesh=mesh,
        in_specs=(
            P("ctx", "head"),
            P("ctx", "head"),
            P("ctx", "head"),
            P("head"),
            P("ctx", "head"),
        ),
        out_specs=(P("ctx", "head"), P("ctx", "head"), P("ctx", "head"), P("ctx", "head")),
        check_vma=False,
    )
```

```python
import functools

import jax
import jax.numpy as jnp
from jax import lax
from jax.experimental import pallas as pl
from jax.experimental.pallas import tpu as pltpu
from jax.sharding import PartitionSpec as P

DH = 128
F32 = jnp.float32
BF16 = jnp.bfloat16
PART = F32
FIRST = 18
NORM_FIRST = 5
SCAN_COST = 10_000_000_000
VMEM_LIMIT = 16 * 1024 * 1024
VMEM_MOST = 60 * 1024 * 1024
SIDE_VMEM = 24 * 1024 * 1024
VMEM = pl.BlockSpec(memory_space=pltpu.VMEM)


def far(x):
    return pltpu.with_memory_space_constraint(x, pltpu.HBM)


NT = (((1,), (1,)), ((), ()))
NN = (((1,), (0,)), ((), ()))
TN = (((0,), (0,)), ((), ()))


def dot(a, b, dims):
    return lax.dot_general(a, b, dims, preferred_element_type=F32)


def params(limit=VMEM_LIMIT):
    return pltpu.CompilerParams(vmem_limit_bytes=limit)


def heads_of(ref):
    return [slice(c, c + DH) for c in range(0, ref.shape[1], DH)]


HBM = pl.BlockSpec(memory_space=pltpu.HBM)


class Mover:
    def __init__(self, sems):
        self.sems = sems
        self.used = 0

    def start(self, src, dst):
        copy = pltpu.make_async_copy(src, dst, self.sems.at[self.used])
        self.used += 1
        copy.start()
        return copy


def chunks_of(ref, step):
    return [slice(r, r + step) for r in range(0, ref.shape[0], step)]


def groups_of(ref, step):
    return [slice(c, c + step) for c in range(0, ref.shape[1], step)]


def outer_kernel(a_hbm, b_hbm, out_hbm, a_ref, b_ref, acc_ref, out_ref, sems, *, step):
    mover = Mover(sems)
    chunks = chunks_of(a_ref, step)
    loads = [
        (mover.start(a_hbm.at[rows], a_ref.at[rows]), mover.start(b_hbm.at[rows], b_ref.at[rows])) for rows in chunks
    ]
    stores = []
    for i, rows in enumerate(chunks):
        for copy in loads[i]:
            copy.wait()
        for h, cols in enumerate(heads_of(a_ref)):
            term = dot(a_ref[rows, cols], b_ref[rows, cols], TN)
            if i > 0:
                term = acc_ref[cols, :] + term
            if i < len(chunks) - 1:
                acc_ref[cols, :] = term
                continue
            out_ref[cols, :] = term.astype(BF16)
            if h % 4 == 3:
                four = slice(cols.stop - 4 * DH, cols.stop)
                stores.append(mover.start(out_ref.at[four], out_hbm.at[four]))
    for copy in stores:
        copy.wait()


def outer(a, b, step):
    rows, width = a.shape
    return pl.pallas_call(
        functools.partial(outer_kernel, step=step),
        in_specs=[HBM] * 2,
        out_specs=HBM,
        out_shape=pltpu.HBM((width, DH), BF16),
        scratch_shapes=[
            pltpu.VMEM((rows, width), BF16),
            pltpu.VMEM((rows, width), BF16),
            pltpu.VMEM((width, DH), F32),
            pltpu.VMEM((width, DH), BF16),
            pltpu.SemaphoreType.DMA((2 * rows // step + width // DH // 4,)),
        ],
        compiler_params=params(VMEM_MOST),
        name="outer",
    )(far(a), far(b))


def ring(count, first):
    return [(first + i) % count for i in range(count)]


def scan_kernel(x_ref, out_ref, *, backward):
    count = x_ref.shape[0]
    total = jnp.zeros(x_ref.shape[1:], F32)
    place = {block: i for i, block in enumerate(ring(count, FIRST))}
    for lap in range(count):
        i = place[count - 1 - lap if backward else lap]
        out_ref[i] = total.astype(BF16)
        total = total + x_ref[i].astype(F32)


def scan(x, backward):
    return pl.pallas_call(
        functools.partial(scan_kernel, backward=backward),
        out_shape=jax.ShapeDtypeStruct(x.shape, BF16),
        cost_estimate=pl.CostEstimate(flops=SCAN_COST, bytes_accessed=SCAN_COST // 300, transcendentals=0),
        compiler_params=params(),
        name="suffix" if backward else "prefix",
    )(x)


def exchange(x, axis):
    return lax.all_to_all(x, axis, 0, 0, axis_index_groups=[ring(x.shape[0], FIRST)])


def gathered(x, axis):
    return lax.all_to_all(x, axis, 0, 0, axis_index_groups=[ring(x.shape[0], NORM_FIRST)])


def keep_lower(x):
    row = lax.broadcasted_iota(jnp.int32, x.shape, 0)
    col = lax.broadcasted_iota(jnp.int32, x.shape, 1)
    return jnp.where(row >= col, x, 0.0)


def keep_upper(x):
    row = lax.broadcasted_iota(jnp.int32, x.shape, 0)
    col = lax.broadcasted_iota(jnp.int32, x.shape, 1)
    return jnp.where(row <= col, x, 0.0)


def lower_parts(a, b):
    half = a.shape[0] // 2
    return (
        keep_lower(dot(a[:half], b[:half], NT)).astype(BF16),
        dot(a[half:], b[:half], NT).astype(BF16),
        keep_lower(dot(a[half:], b[half:], NT)).astype(BF16),
    )


def upper_parts(a, b):
    half = a.shape[0] // 2
    return (
        keep_upper(dot(a[:half], b[:half], NT)).astype(BF16),
        dot(a[:half], b[half:], NT).astype(BF16),
        keep_upper(dot(a[half:], b[half:], NT)).astype(BF16),
    )


def lower_apply(parts, c):
    top, low, last = parts
    half = top.shape[0]
    return dot(top, c[:half], NN), dot(low, c[:half], NN) + dot(last, c[half:], NN)


def upper_apply(parts, c):
    top, high, last = parts
    half = top.shape[0]
    return dot(top, c[:half], NN) + dot(high, c[half:], NN), dot(last, c[half:], NN)


def upper_turned(parts, c):
    top, high, last = parts
    half = top.shape[0]
    return dot(top, c[:half], TN), dot(high, c[:half], TN) + dot(last, c[half:], TN)


def put(ref, cols, pair):
    half = ref.shape[0] // 2
    ref[:half, cols] = pair[0].astype(ref.dtype)
    ref[half:, cols] = pair[1].astype(ref.dtype)


def within_kernel(q_hbm, k_hbm, v_hbm, out_hbm, q_ref, k_ref, v_ref, out_ref, sems, *, step):
    mover = Mover(sems)
    groups = groups_of(q_ref, step)
    pairs = ((q_hbm, q_ref), (k_hbm, k_ref), (v_hbm, v_ref))
    loads = [[mover.start(src.at[:, group], dst.at[:, group]) for src, dst in pairs] for group in groups]
    stores = []
    for i, group in enumerate(groups):
        for copy in loads[i]:
            copy.wait()
        spans = heads_of(q_ref)[i * step // DH : (i + 1) * step // DH]
        parts = [lower_parts(q_ref[:, cols], k_ref[:, cols]) for cols in spans]
        for cols, part in zip(spans, parts):
            put(out_ref, cols, lower_apply(part, v_ref[:, cols]))
        stores.append(mover.start(out_ref.at[:, group], out_hbm.at[:, group]))
    for copy in stores:
        copy.wait()


def within(q, k, v, step):
    return pl.pallas_call(
        functools.partial(within_kernel, step=step),
        in_specs=[HBM] * 3,
        out_specs=HBM,
        out_shape=pltpu.HBM(q.shape, F32),
        scratch_shapes=[pltpu.VMEM(q.shape, BF16)] * 3 + [pltpu.VMEM(q.shape, F32), pltpu.SemaphoreType.DMA((4 * q.shape[1] // step,))],
        compiler_params=params(VMEM_MOST),
        name="within",
    )(far(q), far(k), far(v))


def side_by_side(one, two):
    return jnp.concatenate(
        [
            jnp.concatenate([one, jnp.zeros_like(two)], axis=1),
            jnp.concatenate([jnp.zeros_like(one), two], axis=1),
        ],
        axis=0,
    )


def attend_kernel(a_ref, q_ref, s_ref, cot_ref, gain_ref, att_ref, stat_ref, sq_ref, cr_ref):
    for i, pair in enumerate(groups_of(q_ref, 2 * DH)):
        s = side_by_side(s_ref[pair.start : pair.start + DH, :], s_ref[pair.start + DH : pair.stop, :])
        att = a_ref[:, pair] + dot(q_ref[:, pair], s, NN)
        att_ref[:, pair] = att
        scaled = cot_ref[:, pair].astype(F32) * gain_ref[:, pair].astype(F32)
        for ref, term in ((sq_ref, att * att), (cr_ref, scaled * att)):
            term = term[:, :DH] + term[:, DH:]
            ref[...] = term if i == 0 else ref[...] + term
    chunks = chunks_of(q_ref, DH)
    lines = [jnp.sum(ref[span, :].T, axis=0, keepdims=True) for ref in (sq_ref, cr_ref) for span in chunks]
    lines = jnp.concatenate(lines, axis=0)
    for copy in range(stat_ref.shape[0]):
        stat_ref[copy] = lines


def attend(a, q, s, cot, gain, copies):
    rows, width = q.shape
    return pl.pallas_call(
        attend_kernel,
        out_shape=[
            jax.ShapeDtypeStruct((rows, width), F32),
            jax.ShapeDtypeStruct((copies, 2 * rows // DH, DH), F32),
        ],
        scratch_shapes=[pltpu.VMEM((rows, DH), F32)] * 2,
        compiler_params=params(),
        name="attend",
    )(a, q, s, cot, gain)


def grad_kernel(
    att_ref, cot_ref, gain_ref, q_ref, stat_ref, g_hbm, lg_hbm, n_hbm, g_ref, lg_ref, n_ref, sems, *, total
):
    mover = Mover(sems)
    rows = att_ref.shape[0]
    blocks = rows // DH
    stats = jnp.sum(stat_ref[...], axis=0) / total
    inv = lax.rsqrt(stats[:blocks] + 1e-06)
    pull = inv**3 * stats[blocks:]
    stores = []
    for i, span in enumerate(chunks_of(att_ref, DH)):
        inv_tile = jnp.broadcast_to(inv[i : i + 1], (DH, DH)).T
        pull_tile = jnp.broadcast_to(pull[i : i + 1], (DH, DH)).T
        for cols in heads_of(q_ref):
            gain = gain_ref[:, cols].astype(F32)
            att = att_ref[span, cols]
            scaled = cot_ref[span, cols].astype(F32) * gain
            g_ref[span, cols] = (inv_tile * scaled - att * pull_tile).astype(BF16)
            n_ref[span, cols] = (att * inv_tile * gain).astype(BF16)
        if (i + 1) % 2 == 0:
            rows = slice(span.stop - 2 * DH, span.stop)
            stores.append(mover.start(g_ref.at[rows], g_hbm.at[rows]))
            stores.append(mover.start(n_ref.at[rows], n_hbm.at[rows]))
    for cols in heads_of(q_ref):
        lg_ref[cols, :] = dot(q_ref[:, cols], g_ref[:, cols], TN).astype(BF16)
    stores.append(mover.start(lg_ref, lg_hbm))
    for copy in stores:
        copy.wait()


def grad(att, cot, gain, stats, q, total):
    rows, width = q.shape
    shapes = [(rows, width), (width, DH), (rows, width)]
    return pl.pallas_call(
        functools.partial(grad_kernel, total=total),
        out_specs=[HBM] * 3,
        out_shape=[pltpu.HBM(shape, BF16) for shape in shapes],
        scratch_shapes=[pltpu.VMEM(shape, BF16) for shape in shapes]
        + [pltpu.SemaphoreType.DMA((2 * rows // DH + 1,))],
        cost_estimate=pl.CostEstimate(flops=SCAN_COST, bytes_accessed=SCAN_COST // 300, transcendentals=0),
        compiler_params=params(),
        name="grad",
    )(att, cot, gain, q, stats)


def side_kernel(q_ref, k_ref, v_hbm, g_hbm, s_hbm, *refs, sizes):
    gq_hbm, gk_hbm, gv_hbm, v_ref, g_ref, s_ref, gq_ref, gk_ref, gv_ref, sems = refs
    mover = Mover(sems)
    half = q_ref.shape[0] // 2
    groups = []
    for size in sizes:
        start = groups[-1].stop if groups else 0
        groups.append(slice(start, start + size * DH))
    s_in = mover.start(s_hbm, s_ref)
    pairs = ((g_hbm, g_ref), (v_hbm, v_ref))
    loads = [[mover.start(src.at[:, group], dst.at[:, group]) for src, dst in pairs] for group in groups]
    stores = []
    for i, group in enumerate(groups):
        spans = heads_of(q_ref)[group.start // DH : group.stop // DH]
        if i == 0:
            first = [upper_parts(k_ref[:, cols], q_ref[:, cols]) for cols in spans]
            s_in.wait()
        for copy in loads[i]:
            copy.wait()
        for j, cols in enumerate(spans):
            q, k, v, g = q_ref[:, cols], k_ref[:, cols], v_ref[:, cols], g_ref[:, cols]
            pull = upper_parts(v, g)
            attn = first[j] if i == 0 else upper_parts(k, q)
            rest = dot(g, s_ref[cols, :], NT)
            put(gk_ref, cols, upper_apply(pull, q))
            one, two = upper_turned(pull, k)
            put(gq_ref, cols, (one + rest[:half], two + rest[half:]))
            put(gv_ref, cols, upper_apply(attn, g))
        for src, dst in ((gk_ref, gk_hbm), (gv_ref, gv_hbm), (gq_ref, gq_hbm)):
            stores.append(mover.start(src.at[:, group], dst.at[:, group]))
    for copy in stores:
        copy.wait()


def side(q, k, v, g, s, sizes):
    outs = [pltpu.HBM(q.shape, kind) for kind in (BF16, PART, PART)]
    ins = (q, k, v, g, s)
    return pl.pallas_call(
        functools.partial(side_kernel, sizes=sizes),
        in_specs=[VMEM] * 2 + [HBM] * 3,
        out_specs=[HBM] * len(outs),
        out_shape=outs,
        scratch_shapes=[pltpu.VMEM(x.shape, x.dtype) for x in (*ins[2:], *outs)]
        + [pltpu.SemaphoreType.DMA((1 + 5 * len(sizes),))],
        compiler_params=params(SIDE_VMEM),
        name="side",
    )(q, k, *[far(x) for x in ins[2:]])


def last_kernel(gk_ref, gv_ref, k_ref, v_ref, s_ref, outk_hbm, outv_hbm, outk_ref, outv_ref, sems, *, step):
    mover = Mover(sems)
    stores = []
    for group in groups_of(k_ref, step):
        for cols in heads_of(k_ref)[group.start // DH : group.stop // DH]:
            s = s_ref[cols, :]
            both = dot(jnp.concatenate([v_ref[:, cols], k_ref[:, cols]], axis=1), side_by_side(s.T, s), NN)
            outk_ref[:, cols] = (gk_ref[:, cols] + both[:, :DH]).astype(BF16)
            outv_ref[:, cols] = (gv_ref[:, cols] + both[:, DH:]).astype(BF16)
        stores.append(mover.start(outk_ref.at[:, group], outk_hbm.at[:, group]))
        stores.append(mover.start(outv_ref.at[:, group], outv_hbm.at[:, group]))
    for copy in stores:
        copy.wait()


def last(gk, gv, k, v, s, step):
    rows, width = k.shape
    return pl.pallas_call(
        functools.partial(last_kernel, step=step),
        out_specs=[HBM] * 2,
        out_shape=[pltpu.HBM((rows, width), BF16)] * 2,
        scratch_shapes=[pltpu.VMEM((rows, width), BF16)] * 2 + [pltpu.SemaphoreType.DMA((2 * width // step,))],
        compiler_params=params(),
        name="last",
    )(gk, gv, k, v, s)


def body(queries, keys, values, gain, cotangent):
    rows, width = queries.shape
    count, heads = lax.axis_size("ctx"), lax.axis_size("head")
    gain = gain.reshape(1, width)
    parts = (count, width // count, DH)

    local = exchange(outer(keys, values, 128).reshape(parts), "ctx")
    a = within(queries, keys, values, 256)
    local, a, gain = lax.optimization_barrier((local, a, gain))
    state = exchange(scan(local, False), "ctx").reshape(width, DH)

    att, stats = attend(a, queries, state, cotangent, gain, heads)
    stats = gathered(stats, "head")
    g, local, normed = grad(att, cotangent, gain, stats, queries, width * heads)

    local = exchange(local.reshape(parts), "ctx")
    sides = side(queries, keys, values, g, state, (2, 4, 2))
    local, grad_q, gk, gv = lax.optimization_barrier((local, *sides))
    later = exchange(scan(local, True), "ctx").reshape(width, DH)
    grad_k, grad_v = last(gk, gv, keys, values, later, 256)
    return normed, grad_q, grad_k, grad_v


def solution(mesh):
    return jax.shard_map(
        body,
        mesh=mesh,
        in_specs=(
            P("ctx", "head"),
            P("ctx", "head"),
            P("ctx", "head"),
            P("head"),
            P("ctx", "head"),
        ),
        out_specs=(P("ctx", "head"), P("ctx", "head"), P("ctx", "head"), P("ctx", "head")),
        check_vma=False,
    )
```

```python
import functools

import jax
import jax.numpy as jnp
from jax import lax
from jax.experimental import pallas as pl
from jax.experimental.pallas import tpu as pltpu
from jax.sharding import PartitionSpec as P

DH = 128
F32 = jnp.float32
BF16 = jnp.bfloat16
PART = F32
FIRST = 18
LATER_FIRST = 19
NORM_FIRST = 5
SCAN_COST = 10_000_000_000
VMEM_LIMIT = 16 * 1024 * 1024
VMEM_MOST = 60 * 1024 * 1024
SIDE_VMEM = 24 * 1024 * 1024
VMEM = pl.BlockSpec(memory_space=pltpu.VMEM)


def far(x):
    return pltpu.with_memory_space_constraint(x, pltpu.HBM)


NT = (((1,), (1,)), ((), ()))
NN = (((1,), (0,)), ((), ()))
TN = (((0,), (0,)), ((), ()))


def dot(a, b, dims):
    return lax.dot_general(a, b, dims, preferred_element_type=F32)


def params(limit=VMEM_LIMIT):
    return pltpu.CompilerParams(vmem_limit_bytes=limit)


def heads_of(ref):
    return [slice(c, c + DH) for c in range(0, ref.shape[1], DH)]


HBM = pl.BlockSpec(memory_space=pltpu.HBM)


class Mover:
    def __init__(self, sems):
        self.sems = sems
        self.used = 0

    def start(self, src, dst):
        copy = pltpu.make_async_copy(src, dst, self.sems.at[self.used])
        self.used += 1
        copy.start()
        return copy


def chunks_of(ref, step):
    return [slice(r, r + step) for r in range(0, ref.shape[0], step)]


def groups_of(ref, step):
    return [slice(c, c + step) for c in range(0, ref.shape[1], step)]


def outer_kernel(a_hbm, b_hbm, out_hbm, a_ref, b_ref, acc_ref, out_ref, sems, *, step):
    mover = Mover(sems)
    chunks = chunks_of(a_ref, step)
    loads = [
        (mover.start(a_hbm.at[rows], a_ref.at[rows]), mover.start(b_hbm.at[rows], b_ref.at[rows])) for rows in chunks
    ]
    stores = []
    for i, rows in enumerate(chunks):
        for copy in loads[i]:
            copy.wait()
        for h, cols in enumerate(heads_of(a_ref)):
            term = dot(a_ref[rows, cols], b_ref[rows, cols], TN)
            if i > 0:
                term = acc_ref[cols, :] + term
            if i < len(chunks) - 1:
                acc_ref[cols, :] = term
                continue
            out_ref[cols, :] = term.astype(BF16)
            if h % 4 == 3:
                four = slice(cols.stop - 4 * DH, cols.stop)
                stores.append(mover.start(out_ref.at[four], out_hbm.at[four]))
    for copy in stores:
        copy.wait()


def outer(a, b, step):
    rows, width = a.shape
    return pl.pallas_call(
        functools.partial(outer_kernel, step=step),
        in_specs=[HBM] * 2,
        out_specs=HBM,
        out_shape=pltpu.HBM((width, DH), BF16),
        scratch_shapes=[
            pltpu.VMEM((rows, width), BF16),
            pltpu.VMEM((rows, width), BF16),
            pltpu.VMEM((width, DH), F32),
            pltpu.VMEM((width, DH), BF16),
            pltpu.SemaphoreType.DMA((2 * rows // step + width // DH // 4,)),
        ],
        compiler_params=params(VMEM_MOST),
        name="outer",
    )(far(a), far(b))


def ring(count, first):
    return [(first + i) % count for i in range(count)]


def scan_kernel(x_ref, out_ref, *, backward):
    count = x_ref.shape[0]
    total = jnp.zeros(x_ref.shape[1:], F32)
    place = {block: i for i, block in enumerate(ring(count, LATER_FIRST if backward else FIRST))}
    for lap in range(count):
        i = place[count - 1 - lap if backward else lap]
        out_ref[i] = total.astype(BF16)
        total = total + x_ref[i].astype(F32)


def scan(x, backward):
    return pl.pallas_call(
        functools.partial(scan_kernel, backward=backward),
        out_shape=jax.ShapeDtypeStruct(x.shape, BF16),
        cost_estimate=pl.CostEstimate(flops=SCAN_COST, bytes_accessed=SCAN_COST // 300, transcendentals=0),
        compiler_params=params(),
        name="suffix" if backward else "prefix",
    )(x)


def exchange(x, axis, first):
    return lax.all_to_all(x, axis, 0, 0, axis_index_groups=[ring(x.shape[0], first)])


def gathered(x, axis):
    return lax.all_to_all(x, axis, 0, 0, axis_index_groups=[ring(x.shape[0], NORM_FIRST)])


def keep_lower(x):
    row = lax.broadcasted_iota(jnp.int32, x.shape, 0)
    col = lax.broadcasted_iota(jnp.int32, x.shape, 1)
    return jnp.where(row >= col, x, 0.0)


def keep_upper(x):
    row = lax.broadcasted_iota(jnp.int32, x.shape, 0)
    col = lax.broadcasted_iota(jnp.int32, x.shape, 1)
    return jnp.where(row <= col, x, 0.0)


def lower_parts(a, b):
    half = a.shape[0] // 2
    return (
        keep_lower(dot(a[:half], b[:half], NT)).astype(BF16),
        dot(a[half:], b[:half], NT).astype(BF16),
        keep_lower(dot(a[half:], b[half:], NT)).astype(BF16),
    )


def upper_parts(a, b):
    half = a.shape[0] // 2
    return (
        keep_upper(dot(a[:half], b[:half], NT)).astype(BF16),
        dot(a[:half], b[half:], NT).astype(BF16),
        keep_upper(dot(a[half:], b[half:], NT)).astype(BF16),
    )


def lower_apply(parts, c):
    top, low, last = parts
    half = top.shape[0]
    return dot(top, c[:half], NN), dot(low, c[:half], NN) + dot(last, c[half:], NN)


def upper_apply(parts, c):
    top, high, last = parts
    half = top.shape[0]
    return dot(top, c[:half], NN) + dot(high, c[half:], NN), dot(last, c[half:], NN)


def upper_turned(parts, c):
    top, high, last = parts
    half = top.shape[0]
    return dot(top, c[:half], TN), dot(high, c[:half], TN) + dot(last, c[half:], TN)


def put(ref, cols, pair):
    half = ref.shape[0] // 2
    ref[:half, cols] = pair[0].astype(ref.dtype)
    ref[half:, cols] = pair[1].astype(ref.dtype)


def within_kernel(q_hbm, k_hbm, v_hbm, out_hbm, q_ref, k_ref, v_ref, out_ref, sems, *, step):
    mover = Mover(sems)
    groups = groups_of(q_ref, step)
    pairs = ((q_hbm, q_ref), (k_hbm, k_ref), (v_hbm, v_ref))
    loads = [[mover.start(src.at[:, group], dst.at[:, group]) for src, dst in pairs] for group in groups]
    stores = []
    for i, group in enumerate(groups):
        for copy in loads[i]:
            copy.wait()
        spans = heads_of(q_ref)[i * step // DH : (i + 1) * step // DH]
        parts = [lower_parts(q_ref[:, cols], k_ref[:, cols]) for cols in spans]
        for cols, part in zip(spans, parts):
            put(out_ref, cols, lower_apply(part, v_ref[:, cols]))
        stores.append(mover.start(out_ref.at[:, group], out_hbm.at[:, group]))
    for copy in stores:
        copy.wait()


def within(q, k, v, step):
    return pl.pallas_call(
        functools.partial(within_kernel, step=step),
        in_specs=[HBM] * 3,
        out_specs=HBM,
        out_shape=pltpu.HBM(q.shape, F32),
        scratch_shapes=[pltpu.VMEM(q.shape, BF16)] * 3 + [pltpu.VMEM(q.shape, F32), pltpu.SemaphoreType.DMA((4 * q.shape[1] // step,))],
        compiler_params=params(VMEM_MOST),
        name="within",
    )(far(q), far(k), far(v))


def side_by_side(one, two):
    return jnp.concatenate(
        [
            jnp.concatenate([one, jnp.zeros_like(two)], axis=1),
            jnp.concatenate([jnp.zeros_like(one), two], axis=1),
        ],
        axis=0,
    )


def attend_kernel(a_ref, q_ref, s_ref, cot_ref, gain_ref, att_ref, stat_ref, sq_ref, cr_ref):
    for i, pair in enumerate(groups_of(q_ref, 2 * DH)):
        s = side_by_side(s_ref[pair.start : pair.start + DH, :], s_ref[pair.start + DH : pair.stop, :])
        att = a_ref[:, pair] + dot(q_ref[:, pair], s, NN)
        att_ref[:, pair] = att
        scaled = cot_ref[:, pair].astype(F32) * gain_ref[:, pair].astype(F32)
        for ref, term in ((sq_ref, att * att), (cr_ref, scaled * att)):
            term = term[:, :DH] + term[:, DH:]
            ref[...] = term if i == 0 else ref[...] + term
    chunks = chunks_of(q_ref, DH)
    lines = [jnp.sum(ref[span, :].T, axis=0, keepdims=True) for ref in (sq_ref, cr_ref) for span in chunks]
    lines = jnp.concatenate(lines, axis=0)
    for copy in range(stat_ref.shape[0]):
        stat_ref[copy] = lines


def attend(a, q, s, cot, gain, copies):
    rows, width = q.shape
    return pl.pallas_call(
        attend_kernel,
        out_shape=[
            jax.ShapeDtypeStruct((rows, width), F32),
            jax.ShapeDtypeStruct((copies, 2 * rows // DH, DH), F32),
        ],
        scratch_shapes=[pltpu.VMEM((rows, DH), F32)] * 2,
        compiler_params=params(),
        name="attend",
    )(a, q, s, cot, gain)


def grad_kernel(
    att_ref, cot_ref, gain_ref, q_ref, stat_ref, g_hbm, lg_hbm, n_hbm, g_ref, lg_ref, n_ref, sems, *, total
):
    mover = Mover(sems)
    rows = att_ref.shape[0]
    blocks = rows // DH
    stats = jnp.sum(stat_ref[...], axis=0) / total
    inv = lax.rsqrt(stats[:blocks] + 1e-06)
    pull = inv**3 * stats[blocks:]
    stores = []
    for i, span in enumerate(chunks_of(att_ref, DH)):
        inv_tile = jnp.broadcast_to(inv[i : i + 1], (DH, DH)).T
        pull_tile = jnp.broadcast_to(pull[i : i + 1], (DH, DH)).T
        for cols in heads_of(q_ref):
            gain = gain_ref[:, cols].astype(F32)
            att = att_ref[span, cols]
            scaled = cot_ref[span, cols].astype(F32) * gain
            g_ref[span, cols] = (inv_tile * scaled - att * pull_tile).astype(BF16)
            n_ref[span, cols] = (att * inv_tile * gain).astype(BF16)
        if (i + 1) % 2 == 0:
            rows = slice(span.stop - 2 * DH, span.stop)
            stores.append(mover.start(g_ref.at[rows], g_hbm.at[rows]))
            stores.append(mover.start(n_ref.at[rows], n_hbm.at[rows]))
    for cols in heads_of(q_ref):
        lg_ref[cols, :] = dot(q_ref[:, cols], g_ref[:, cols], TN).astype(BF16)
    stores.append(mover.start(lg_ref, lg_hbm))
    for copy in stores:
        copy.wait()


def grad(att, cot, gain, stats, q, total):
    rows, width = q.shape
    shapes = [(rows, width), (width, DH), (rows, width)]
    return pl.pallas_call(
        functools.partial(grad_kernel, total=total),
        out_specs=[HBM] * 3,
        out_shape=[pltpu.HBM(shape, BF16) for shape in shapes],
        scratch_shapes=[pltpu.VMEM(shape, BF16) for shape in shapes]
        + [pltpu.SemaphoreType.DMA((2 * rows // DH + 1,))],
        cost_estimate=pl.CostEstimate(flops=SCAN_COST, bytes_accessed=SCAN_COST // 300, transcendentals=0),
        compiler_params=params(),
        name="grad",
    )(att, cot, gain, q, stats)


def side_kernel(q_ref, k_ref, v_hbm, g_hbm, s_hbm, *refs, sizes):
    gq_hbm, gk_hbm, gv_hbm, v_ref, g_ref, s_ref, gq_ref, gk_ref, gv_ref, sems = refs
    mover = Mover(sems)
    half = q_ref.shape[0] // 2
    groups = []
    for size in sizes:
        start = groups[-1].stop if groups else 0
        groups.append(slice(start, start + size * DH))
    s_in = mover.start(s_hbm, s_ref)
    pairs = ((g_hbm, g_ref), (v_hbm, v_ref))
    loads = [[mover.start(src.at[:, group], dst.at[:, group]) for src, dst in pairs] for group in groups]
    stores = []
    for i, group in enumerate(groups):
        spans = heads_of(q_ref)[group.start // DH : group.stop // DH]
        if i == 0:
            first = [upper_parts(k_ref[:, cols], q_ref[:, cols]) for cols in spans]
            s_in.wait()
        for copy in loads[i]:
            copy.wait()
        for j, cols in enumerate(spans):
            q, k, v, g = q_ref[:, cols], k_ref[:, cols], v_ref[:, cols], g_ref[:, cols]
            pull = upper_parts(v, g)
            attn = first[j] if i == 0 else upper_parts(k, q)
            rest = dot(g, s_ref[cols, :], NT)
            put(gk_ref, cols, upper_apply(pull, q))
            one, two = upper_turned(pull, k)
            put(gq_ref, cols, (one + rest[:half], two + rest[half:]))
            put(gv_ref, cols, upper_apply(attn, g))
        for src, dst in ((gk_ref, gk_hbm), (gv_ref, gv_hbm), (gq_ref, gq_hbm)):
            stores.append(mover.start(src.at[:, group], dst.at[:, group]))
    for copy in stores:
        copy.wait()


def side(q, k, v, g, s, sizes):
    outs = [pltpu.HBM(q.shape, kind) for kind in (BF16, PART, PART)]
    ins = (q, k, v, g, s)
    return pl.pallas_call(
        functools.partial(side_kernel, sizes=sizes),
        in_specs=[VMEM] * 2 + [HBM] * 3,
        out_specs=[HBM] * len(outs),
        out_shape=outs,
        scratch_shapes=[pltpu.VMEM(x.shape, x.dtype) for x in (*ins[2:], *outs)]
        + [pltpu.SemaphoreType.DMA((1 + 5 * len(sizes),))],
        compiler_params=params(SIDE_VMEM),
        name="side",
    )(q, k, *[far(x) for x in ins[2:]])


def last_kernel(gk_ref, gv_ref, k_ref, v_ref, s_ref, outk_hbm, outv_hbm, outk_ref, outv_ref, sems, *, step):
    mover = Mover(sems)
    stores = []
    for group in groups_of(k_ref, step):
        for cols in heads_of(k_ref)[group.start // DH : group.stop // DH]:
            s = s_ref[cols, :]
            both = dot(jnp.concatenate([v_ref[:, cols], k_ref[:, cols]], axis=1), side_by_side(s.T, s), NN)
            outk_ref[:, cols] = (gk_ref[:, cols] + both[:, :DH]).astype(BF16)
            outv_ref[:, cols] = (gv_ref[:, cols] + both[:, DH:]).astype(BF16)
        stores.append(mover.start(outk_ref.at[:, group], outk_hbm.at[:, group]))
        stores.append(mover.start(outv_ref.at[:, group], outv_hbm.at[:, group]))
    for copy in stores:
        copy.wait()


def last(gk, gv, k, v, s, step):
    rows, width = k.shape
    return pl.pallas_call(
        functools.partial(last_kernel, step=step),
        out_specs=[HBM] * 2,
        out_shape=[pltpu.HBM((rows, width), BF16)] * 2,
        scratch_shapes=[pltpu.VMEM((rows, width), BF16)] * 2 + [pltpu.SemaphoreType.DMA((2 * width // step,))],
        compiler_params=params(),
        name="last",
    )(gk, gv, k, v, s)


def body(queries, keys, values, gain, cotangent):
    rows, width = queries.shape
    count, heads = lax.axis_size("ctx"), lax.axis_size("head")
    gain = gain.reshape(1, width)
    parts = (count, width // count, DH)

    local = exchange(outer(keys, values, 128).reshape(parts), "ctx", FIRST)
    a = within(queries, keys, values, 256)
    local, a, gain = lax.optimization_barrier((local, a, gain))
    state = exchange(scan(local, False), "ctx", FIRST).reshape(width, DH)

    att, stats = attend(a, queries, state, cotangent, gain, heads)
    stats = gathered(stats, "head")
    g, local, normed = grad(att, cotangent, gain, stats, queries, width * heads)

    local = exchange(local.reshape(parts), "ctx", LATER_FIRST)
    sides = side(queries, keys, values, g, state, (2, 4, 2))
    local, grad_q, gk, gv = lax.optimization_barrier((local, *sides))
    later = exchange(scan(local, True), "ctx", LATER_FIRST).reshape(width, DH)
    grad_k, grad_v = last(gk, gv, keys, values, later, 256)
    return normed, grad_q, grad_k, grad_v


def solution(mesh):
    return jax.shard_map(
        body,
        mesh=mesh,
        in_specs=(
            P("ctx", "head"),
            P("ctx", "head"),
            P("ctx", "head"),
            P("head"),
            P("ctx", "head"),
        ),
        out_specs=(P("ctx", "head"), P("ctx", "head"), P("ctx", "head"), P("ctx", "head")),
        check_vma=False,
    )
```
